32 devices in a mesh: clips: 8 (over y, x, core), mlp: 4 (over z).
Axes of the slice: x: 2, y: 2, z: 4, core: 2. Of those that a mesh axis runs over, the one named last changes fastest.
Arguments:
- tokens: bfloat16 [32768, 768], P(('clips', 'mlp')), may hold values from -6 to 6
- clip_lengths: int32 [32, 4], P(('clips', 'mlp')), may hold values from 1 to 512, 1024 in all within a row
- visible: int32 [32768], P(('clips', 'mlp')), may hold values 0 or 1
- ln1_gain: bfloat16 [768], P('mlp'), may hold values from 0.5 to 1.5
- ln1_bias: bfloat16 [768], P('mlp'), may hold values from -1.25 to 1.25
- w_qkv: bfloat16 [768, 2304], P('clips', 'mlp'), may hold values from -0.3125 to 0.3125
- b_qv: bfloat16 [1536], P('mlp'), may hold values from -1.25 to 1.25
- w_out: bfloat16 [768, 768], P('clips', 'mlp'), may hold values from -1.75 to 1.75
- b_out: bfloat16 [768], P('mlp'), may hold values from -1.25 to 1.25
- ln2_gain: bfloat16 [768], P('mlp'), may hold values from 0.5 to 1.5
- ln2_bias: bfloat16 [768], P('mlp'), may hold values from -1.25 to 1.25
- w_fc1: bfloat16 [768, 3072], P('clips', 'mlp'), may hold values from -0.21875 to 0.21875
- b_fc1: bfloat16 [3072], P('mlp'), may hold values from -1.25 to 1.25
- w_fc2: bfloat16 [3072, 768], P('mlp', 'clips'), may hold values from -0.109375 to 0.109375
- b_fc2: bfloat16 [768], P('mlp'), may hold values from -1.25 to 1.25
- cotangent: bfloat16 [32768, 768], P(('clips', 'mlp')), may hold values from -12 to 12
Outputs:
- block_out: bfloat16 [32768, 768], P(('clips', 'mlp'))
- input_grad: float32 [32768, 768], P(('clips', 'mlp'))
- grad_ln1_gain: float32 [768], P('mlp')
- grad_ln1_bias: float32 [768], P('mlp')
- grad_w_qkv: float32 [768, 2304], P('clips', 'mlp')
- grad_b_qv: float32 [1536], P('mlp')
- grad_w_out: float32 [768, 768], P('clips', 'mlp')
- grad_b_out: float32 [768], P('mlp')
- grad_ln2_gain: float32 [768], P('mlp')
- grad_ln2_bias: float32 [768], P('mlp')
- grad_w_fc1: float32 [768, 3072], P('clips', 'mlp')
- grad_b_fc1: float32 [3072], P('mlp')
- grad_w_fc2: float32 [3072, 768], P('mlp', 'clips')
- grad_b_fc2: float32 [768], P('mlp')
The draws below stay inside these ranges and needn't reach their ends.
Inputs may be any that keep to these rules, and one draw needn't show every extreme that they name: `clip_lengths`: each row lists the kept token counts of the 4 clips packed into one block of 1024 rows; a row sums to 1024 and its largest entry is 512.
All inputs are finite; a program needn't handle non-finite values. No bound on the sum of `visible` on one device may be relied on, other than what follows from the above.
Results may differ from the reference program's by a relative error of at most 0.015.
Values may be sent and summed in bfloat16 or wider, within the bound.
A program may use at most 192 MiB of HBM per device.

```python
import math
import jax
import jax.numpy as jnp
import numpy as np
from jax import lax

D = 768
HEADS = 12
HEAD_DIM = 64
FF = 3072
TOK_DEV = 1024
CLIPS_DEV = 4
LONGEST = 512
TOKENS = 32768
N_MLP = 4
DEVICES = 32


def plant(values, rng, low, top_value):
    shape = values.shape
    place = [jax.random.randint(jax.random.fold_in(rng, axis), (), 0, shape[axis]) for axis in range(len(shape))]
    values = values.at[tuple(place)].set(low)
    longest = shape.index(max(shape))
    place[longest] = (place[longest] + 1) % shape[longest]
    return values.at[tuple(place)].set(top_value)


def with_spikes(values, key, source, target, shards_of, factor):
    def block_of(position):
        return (jnp.arange(values.shape[position]) // (values.shape[position] // shards_of)).reshape((-1,) + (1,) * (values.ndim - 1 - position))

    one_side = jax.random.permutation(key, shards_of)[block_of(target)]
    far = (block_of(target) + shards_of // 2) % shards_of
    return jnp.where((block_of(source) == one_side) | (block_of(source) == far), factor * values, values)


def steps_of(stream_key, extent, cuts, least, high):
    level, own = 1.0, jax.random.fold_in(stream_key, 6)
    for dim, blocks in cuts:
        steps = jnp.exp(jax.random.uniform(jax.random.fold_in(own, dim), (blocks,), jnp.float32, least / len(cuts), high / len(cuts)))
        level = level * jnp.repeat(steps, extent[dim] // blocks).reshape([-1 if axis == dim else 1 for axis in range(len(extent))])
    return level


def length_profile(amount, total, bound, skew):
    weights = [(1 << 20) // math.isqrt(standing ** skew) + 1 for standing in range(2, amount + 1)]
    surplus, holding = total - bound - (amount - 1), [1] * (amount - 1)
    while surplus > 0:
        free = [i for i in range(amount - 1) if holding[i] < bound]
        mass, left = sum([weights[i] for i in free]), surplus
        for i in free:
            addition = min(bound - holding[i], max(1, left * weights[i] // mass), surplus)
            holding[i] = holding[i] + addition
            surplus = surplus - addition
    return np.array([bound] + holding)


def uneven_parts(rng, amount, total, limit, skew):
    if amount == 2:
        one = jax.random.randint(rng, (), max(1, total - limit), min(limit, total - 1) + 1)
        return jnp.stack([one, total - one])
    sizes = jnp.asarray(length_profile(amount, total, limit, skew), jnp.int32)
    couples = (amount - 1) // 2
    source_of, taker = sizes[1:1 + 2 * couples:2], sizes[2:2 + 2 * couples:2]
    slack = jnp.minimum(source_of - 1, limit - taker)
    passed = jax.random.randint(jax.random.fold_in(rng, 1), (couples,), 0, 1 << 20) % (slack + 1)
    sizes = sizes.at[1:1 + 2 * couples:2].set(source_of - passed).at[2:2 + 2 * couples:2].set(taker + passed)
    return sizes[jax.random.permutation(jax.random.fold_in(rng, 2), amount)]


def bell_draw(stream_key, shape, deviation, bound, pieces=(), held_as=jnp.bfloat16):
    values = jax.random.normal(stream_key, shape, jnp.float32) * deviation
    if len(pieces) > 0:
        values = steps_of(stream_key, shape, pieces, -0.22, 0.18) * values
    return jnp.clip(values, min=-bound, max=bound).astype(held_as)


def gaussian_with(own_key, dims, scale, bound, cuts, heavy, kind=jnp.bfloat16):
    drawn = scale * jax.random.normal(own_key, dims, jnp.float32)
    if cuts:
        drawn = drawn * steps_of(own_key, dims, cuts, -0.22, 0.18)
    return jnp.clip(with_spikes(drawn, jax.random.fold_in(own_key, 3), *heavy), -bound, bound).astype(kind)


def setup_inputs(seed: int = 0) -> dict:
    key_of = jax.random.split(jax.random.key(seed), 17)
    tokens = bell_draw(key_of[0], (TOKENS, D), 1.0, 6.0, ((0, 32),))
    clip_lengths = jax.vmap(lambda own: uneven_parts(own, CLIPS_DEV, TOK_DEV, LONGEST, 2))(jax.random.split(key_of[1], DEVICES)).reshape((DEVICES, CLIPS_DEV)).astype(jnp.int32)
    visible = plant((jax.random.randint(key_of[2], (TOKENS,), 0, 5) < 4).astype(jnp.int32), jax.random.fold_in(key_of[2], 1), 0, 1)
    ln1_gain = jnp.clip(1.0 + 0.1 * jax.random.normal(key_of[3], (D,), jnp.float32), 0.5, 1.5).astype(jnp.bfloat16)
    ln1_bias = bell_draw(key_of[4], (D,), 0.2, 1.25, ((0, 4),))
    w_qkv = bell_draw(key_of[5], (D, 3 * D), (D // 2) ** -0.5, 0.3125, ((0, 8), (1, 4)))
    b_qv = bell_draw(key_of[6], (2 * D,), 0.2, 1.25, ((0, 4),))
    w_out = bell_draw(key_of[7], (D, D), (max(1, 16 * D // TOK_DEV)) ** -0.5, 1.75, ((0, 8), (1, 4)))
    b_out = bell_draw(key_of[8], (D,), 0.2, 1.25, ((0, 4),))
    ln2_gain = jnp.clip(1.0 + 0.1 * jax.random.normal(key_of[9], (D,), jnp.float32), 0.5, 1.5).astype(jnp.bfloat16)
    ln2_bias = bell_draw(key_of[10], (D,), 0.2, 1.25, ((0, 4),))
    w_fc1 = bell_draw(key_of[11], (D, FF), D ** -0.5, 0.21875, ((0, 8), (1, 4)))
    b_fc1 = bell_draw(key_of[12], (FF,), 0.2, 1.25, ((0, 4),))
    w_fc2 = bell_draw(key_of[13], (FF, D), FF ** -0.5, 0.109375, ((0, 4), (1, 8)))
    b_fc2 = bell_draw(key_of[14], (D,), 0.2, 1.25, ((0, 4),))
    cotangent = gaussian_with(key_of[15], (TOKENS, D), 1.0, 12.0, ((0, 32),), (0, 1, 32, 2.75))
    return dict(tokens=tokens, clip_lengths=clip_lengths, visible=visible, ln1_gain=ln1_gain, ln1_bias=ln1_bias, w_qkv=w_qkv, b_qv=b_qv, w_out=w_out, b_out=b_out, ln2_gain=ln2_gain, ln2_bias=ln2_bias, w_fc1=w_fc1, b_fc1=b_fc1, w_fc2=w_fc2, b_fc2=b_fc2, cotangent=cotangent)


@jax.custom_vjp
def low(v):
    return lax.optimization_barrier(v.astype(jnp.bfloat16)).astype(jnp.float32)

@jax.custom_vjp
def low_back(v):
    return v

def low_keep(v):
    return (low(v), None)

def low_pass(kept, grad):
    return (grad,)

def back_keep(v):
    return (v, None)

def back_low(kept, grad):
    return (low(grad),)
low.defvjp(low_keep, low_pass)
low_back.defvjp(back_keep, back_low)
NORM_EPS = 1e-06
MASKED = -1000000000.0
HIGH = lax.Precision.HIGHEST

def norm_rows(values, gain, shift):
    mean = lax.optimization_barrier(jnp.mean(values, axis=-1, keepdims=True))
    centred = values - mean
    spread = lax.optimization_barrier(jnp.mean(centred * centred, axis=-1, keepdims=True))
    return centred * lax.rsqrt(spread + NORM_EPS) * gain + shift

def clip_mask(lengths_row, visible_row):
    count = visible_row.shape[0]
    ends = jnp.cumsum(lengths_row)
    places = jnp.arange(count, dtype=jnp.int32)
    clip_of = lax.optimization_barrier(jnp.sum((places[:, None] >= ends[None, :]).astype(jnp.int32), axis=1))
    same = clip_of[:, None] == clip_of[None, :]
    seen = (visible_row[None, :] == 1) | (places[:, None] == places[None, :])
    return same & seen

def matmul(left, right):
    return jnp.dot(left, right, precision=HIGH)

def attend_block(inputs):
    query, key, value, lengths_row, visible_row = inputs
    allowed = clip_mask(lengths_row, visible_row)
    q_heads = query.reshape(TOK_DEV, HEADS, HEAD_DIM)
    k_heads = key.reshape(TOK_DEV, HEADS, HEAD_DIM)
    v_heads = value.reshape(TOK_DEV, HEADS, HEAD_DIM)
    scores = jnp.einsum('qhd,khd->hqk', q_heads, k_heads, precision=HIGH) * HEAD_DIM ** (-0.5)
    scores = low_back(jnp.where(allowed[None], scores, MASKED))
    probs = low(jax.nn.softmax(scores, axis=-1))
    out = jnp.einsum('hqk,khd->qhd', probs, v_heads, precision=HIGH)
    return out.reshape(TOK_DEV, D)

def reference(tokens, clip_lengths, visible, ln1_gain, ln1_bias, w_qkv, b_qv, w_out, b_out, ln2_gain, ln2_bias, w_fc1, b_fc1, w_fc2, b_fc2, cotangent):
    total_rows = tokens.shape[0]
    blocks = total_rows // TOK_DEV
    visible_rows = visible.reshape(blocks, TOK_DEV)

    def forward(inputs, gain1, shift1, wqkv, bqv, wout, bout, gain2, shift2, wfc1, bfc1, wfc2, bfc2):
        h1 = low(norm_rows(inputs, gain1, shift1))
        proj = matmul(h1, wqkv)
        query = low(low_back(proj[:, :D] + bqv[:D]))
        key = low(low_back(proj[:, D:2 * D]))
        value = low(low_back(proj[:, 2 * D:] + bqv[D:]))
        shape3 = (blocks, TOK_DEV, D)
        attended = lax.map(jax.checkpoint(attend_block), (query.reshape(shape3), key.reshape(shape3), value.reshape(shape3), clip_lengths, visible_rows))
        attended = low(low_back(attended.reshape(total_rows, D)))
        branch_a = low_back(matmul(attended, wout) + bout)
        mixed = inputs + branch_a
        h2 = low(norm_rows(mixed, gain2, shift2))
        share = FF // N_MLP
        branch = jnp.zeros((total_rows, D), jnp.float32)
        for group in range(N_MLP):
            first = group * share
            last = first + share
            pre = low_back(matmul(low_back(h2), wfc1[:, first:last]) + bfc1[first:last])
            hidden = low(jax.nn.gelu(pre, approximate=False))
            branch = branch + low(matmul(hidden, wfc2[first:last]))
        return mixed + branch + bfc2
    primal = (tokens.astype(jnp.float32), ln1_gain.astype(jnp.float32), ln1_bias.astype(jnp.float32), w_qkv.astype(jnp.float32), b_qv.astype(jnp.float32), w_out.astype(jnp.float32), b_out.astype(jnp.float32), ln2_gain.astype(jnp.float32), ln2_bias.astype(jnp.float32), w_fc1.astype(jnp.float32), b_fc1.astype(jnp.float32), w_fc2.astype(jnp.float32), b_fc2.astype(jnp.float32))
    result, pullback = jax.vjp(forward, *primal)
    grads = pullback(cotangent.astype(jnp.float32))
    return (result.astype(jnp.bfloat16), grads[0], grads[1], grads[2], grads[3], grads[4], grads[5], grads[6], grads[7], grads[8], grads[9], grads[10], grads[11], grads[12])
```

```python
import functools

import jax
import jax.numpy as jnp
from jax import lax
from jax.experimental import pallas as pl
from jax.experimental.pallas import tpu as pltpu
from jax.sharding import PartitionSpec as P

F32 = jnp.float32
BF = jnp.bfloat16
MESH = pl.DeviceIdType.MESH
HEADS = 12
HEAD_DIM = 64
NORM_EPS = 1e-06
MASKED = -1000000000.0
D = 768
TOK = 1024
HALF = 512
QW = 1152
FC0 = 2 * QW + D
FCW = 2048
COLS = FC0 + 3 * FCW
BACK = 3 * FCW + D
R = 256


def dot(a, b):
    return jnp.dot(a, b, preferred_element_type=F32)


def dot_nt(a, b):
    return lax.dot_general(a, b, (((1,), (1,)), ((), ())), preferred_element_type=F32)


def tile_rows(i, size):
    return pl.ds(pl.multiple_of(i * size, size), size)


def lanes_at(start, size):
    return pl.ds(pl.multiple_of(start, 128), size)


def loop(count, body):
    def step(i, carry):
        body(i)
        return carry

    lax.fori_loop(0, count, step, 0)


def norm_parts(x):
    mean = jnp.mean(x, axis=-1, keepdims=True)
    centred = x - mean
    spread = jnp.mean(centred * centred, axis=-1, keepdims=True)
    r = lax.rsqrt(spread + NORM_EPS)
    return centred * r, r


def norm_back(dh, xhat, r, gain):
    e = dh * gain
    m1 = jnp.mean(e, axis=-1, keepdims=True)
    m2 = jnp.mean(e * xhat, axis=-1, keepdims=True)
    return r * (e - m1 - xhat * m2)


def gelu_parts(a):
    e = jnp.exp(a * a * -0.5)
    t = 1.0 / (1.0 + jnp.abs(a) * (0.3275911 * 0.7071067811865476))
    poly = t * (
        0.254829592
        + t * (-0.284496736 + t * (1.421413741 + t * (-1.453152027 + t * 1.061405429)))
    )
    half = 0.5 * poly * e
    phi = jnp.where(a < 0, half, 1.0 - half)
    return a * phi, phi + a * e * 0.3989422804014327


def longest_start(lens):
    n0, n1, n2, n3 = lens[0, 0], lens[0, 1], lens[0, 2], lens[0, 3]
    top = jnp.maximum(jnp.maximum(n0, n1), jnp.maximum(n2, n3))
    start = jnp.where(
        n0 == top, 0, jnp.where(n1 == top, n0, jnp.where(n2 == top, n0 + n1, n0 + n1 + n2))
    )
    return start, (n0, n0 + n1, n0 + n1 + n2)


def one_hot_cols(rows, cols, shift):
    r = lax.broadcasted_iota(jnp.int32, (rows, cols), 0)
    c = lax.broadcasted_iota(jnp.int32, (rows, cols), 1)
    return (r == c + shift).astype(BF)


class Copies:
    def __init__(self, send, recv):
        self.send, self.recv, self.n, self.open = send, recv, 0, []

    def start(self, src, dst, device):
        k = self.n
        self.n += 1
        copy = pltpu.make_async_remote_copy(
            src_ref=src,
            dst_ref=dst,
            send_sem=self.send.at[k],
            recv_sem=self.recv.at[k],
            device_id=device,
            device_id_type=MESH,
        )
        copy.start()
        self.open.append(copy)
        return copy

    def drain(self):
        for copy in self.open:
            copy.wait_send()
        self.open = []


def places():
    c = lax.axis_index("clips")
    m = lax.axis_index("mlp")
    core = lax.rem(c, 2)
    x = lax.rem(lax.div(c, 2), 2)
    y = lax.div(c, 4)
    cs = c + 1 - 2 * core
    cx = c + 2 - 4 * x
    cy = c + 4 - 8 * y
    cd = cx + 4 - 8 * y
    zs = [lax.rem(m + d, 4) for d in (1, 2, 3)]
    return c, m, core, cs, cx, cy, cd, zs


def piece(at, width, half=None):
    if half is None:
        return at, width
    first = (width // 2 + 127) // 128 * 128
    return (at, first) if half == 0 else (at + first, width - first)


def rows_of(c):
    return pl.ds(pl.multiple_of(c * 96, 16), 96)


def mega(comm, *refs):
    refs = list(refs)

    def take(n):
        out = refs[:n]
        del refs[:n]
        return out

    lens, tok_in, cot_in, vis = take(4)
    if comm:
        wq_in, wo_in, w1_in, w2_in, vp_in = take(5)
    else:
        g_in, vpg_in = take(2)
    bo_out, ig_out = take(2)
    if comm:
        gq_out, go_out, g1_out, g2_out, vg_out = take(5)
    else:
        dg_out, vg_out = take(2)
    (G, TK, CT, T1, T2, T3, HB, O, QA, QB, X2, YA, DH, H, DA, BIAS, LSE, VG, VPG, lsem) = take(20)
    if comm:
        ZA, ZB, ZO, SF, RS, RD, RX, RY, RZ, VB, VR, ssem, rsem = take(13)
    QS = (QA, QB)

    tok_copy = pltpu.make_async_copy(tok_in, H.at[:, pl.ds(0, D)], lsem.at[0])
    cot_copy = pltpu.make_async_copy(cot_in, DA.at[:, pl.ds(0, D)], lsem.at[1])
    tok_copy.start()
    cot_copy.start()

    todo = []

    def serve(n=1):
        for _ in range(n):
            if todo:
                todo.pop(0)()

    if comm:
        c, m, core, cs, cx, cy, cd, zs = places()
        barrier = pltpu.get_barrier_semaphore()
        partners = [(cs, m), (cx, m), (cy, m)] + [(c, z) for z in zs]
        for p in partners:
            pl.semaphore_signal(barrier, inc=1, device_id=p, device_id_type=MESH)
        mine = rows_of(c)

        off_a = jnp.where(m == 0, 0, jnp.where(m == 1, 192, jnp.where(m == 2, 384, -192)))
        off_b = jnp.where(m == 0, 384, jnp.where(m == 1, -192, jnp.where(m == 2, 0, 192)))
        off_o = jnp.where(lax.rem(m, 2) == 0, 0, -64)
        wq = wq_in[...]
        ZA[m] = dot(wq, one_hot_cols(576, 384, off_a)).astype(BF)
        ZB[m] = dot(wq, one_hot_cols(576, 384, off_b)).astype(BF)
        ZO[m] = dot(wo_in[...], one_hot_cols(192, 256, off_o)).astype(BF)
        SF[:, 0:D] = w1_in[...]
        SF[:, D : 2 * D] = dot_nt(one_hot_cols(96, 96, 0), w2_in[...]).astype(BF)
        VPG[m] = vp_in[...]
        for j in range(3):
            for s in range(2):
                G[mine, lanes_at(FC0 + j * FCW + s * 1024 + m * 256, 256)] = SF[
                    :, s * D + j * 256 : s * D + (j + 1) * 256
                ]
        pl.semaphore_wait(barrier, 6)
        copies = Copies(ssem, rsem)

        z_of = {}

        def send_vec():
            z_of["v"] = [copies.start(VPG.at[m], VPG.at[m], (c, z)) for z in zs]

        def send_z(name):
            if name in ("a", "b", "o"):
                buf = {"a": ZA, "b": ZB, "o": ZO}[name]
                z_of[name] = [copies.start(buf.at[m], buf.at[m], (c, z)) for z in zs]
            else:
                got = []
                for s in range(2):
                    at = lanes_at(FC0 + name * FCW + s * 1024 + m * 256, 256)
                    got += [
                        copies.start(
                            SF.at[:, pl.ds(s * D + name * 256, 256)], G.at[mine, at], (c, z)
                        )
                        for z in zs
                    ]
                z_of[name] = got

        spans = {"a": (0, QW), "b": (QW, QW), "o": (2 * QW, D)}
        for j in range(3):
            spans[j] = (FC0 + j * FCW, FCW)
        got_of = {}

        def merge(name):
            for k in z_of[name]:
                k.wait_recv()
            if name == "a":
                G[mine, 0:384] = ZA[0]
                G[mine, 384:768] = ZA[1]
                G[mine, 768:QW] = ZA[2] + ZA[3]
            elif name == "b":
                G[mine, QW : QW + 384] = ZB[0] + ZB[1]
                G[mine, QW + 384 : QW + 768] = ZB[2]
                G[mine, QW + 768 : 2 * QW] = ZB[3]
            elif name == "o":
                b = 2 * QW
                for h in range(2):
                    lo, hi = ZO[2 * h], ZO[2 * h + 1]
                    G[mine, b + 384 * h : b + 384 * h + 128] = lo[:, 0:128]
                    G[mine, b + 384 * h + 128 : b + 384 * h + 256] = lo[:, 128:256] + hi[:, 0:128]
                    G[mine, b + 384 * h + 256 : b + 384 * h + 384] = hi[:, 128:256]

        def part(name, block, half=None):
            at, width = piece(*spans[name], half)
            return G.at[rows_of(block), pl.ds(at, width)]

        def step_xy(name):
            merge(name)
            mx = copies.start(part(name, c), part(name, c), (cx, m))
            my = copies.start(part(name, c), part(name, c), (cy, m))
            ms = copies.start(part(name, c), part(name, c), (cs, m))
            got_of[name] = [mx, my, ms]

        def step_diag(name):
            mx, my, ms = got_of[name]
            mx.wait_recv()
            dy = copies.start(part(name, cx, 0), part(name, cx, 0), (cy, m))
            s1 = copies.start(part(name, cx), part(name, cx), (cs, m))
            my.wait_recv()
            dx = copies.start(part(name, cy, 1), part(name, cy, 1), (cx, m))
            s2 = copies.start(part(name, cy), part(name, cy), (cs, m))
            got_of[name] = [dy, dx, ms, s1, s2]

        def step_sib(name):
            dy, dx, ms, s1, s2 = got_of[name]
            dy.wait_recv()
            dx.wait_recv()
            s3 = copies.start(part(name, cd), part(name, cd), (cs, m))
            got_of[name] = [ms, s1, s2, s3]

        def step_done(name):
            for k in got_of[name]:
                k.wait_recv()

        def on(f, *names):
            def run():
                for n in names:
                    f(n)

            return run

        send_vec()
        send_z("a")
        send_z("b")
    else:
        g_copy = pltpu.make_async_copy(g_in, G, lsem.at[2])
        g_copy.start()
        VPG[...] = vpg_in[...]

    start, ends = longest_start(lens)
    tok_copy.wait()
    cot_copy.wait()
    vis8 = vis[...].astype(F32).astype(BF)

    def roll_tile(i):
        rows = tile_rows(i, R)
        place = lax.broadcasted_iota(jnp.int32, (R, 1), 0) + i * R + start
        place = jnp.where(place >= TOK, place - TOK, place)
        perm = (lax.broadcasted_iota(jnp.int32, (R, TOK), 1) == place).astype(BF)
        TK[rows, :] = dot(perm, H[:, 0:D]).astype(BF)
        CT[rows, :] = dot(perm, DA[:, 0:D]).astype(BF)
        seen = dot_nt(perm, vis8)[:, 0:1]
        clip = sum((place >= e).astype(jnp.int32) for e in ends)
        key = lax.broadcasted_iota(jnp.int32, (R, 1), 0) + lax.rem(i, 2) * R
        spot = lax.broadcasted_iota(jnp.int32, (1, HALF), 1)
        far = spot + lax.div(i, 2) * HALF + start
        far = jnp.where(far >= TOK, far - TOK, far)
        clip_q = sum((far >= e).astype(jnp.int32) for e in ends)
        allowed = (clip == clip_q) & ((seen > 0.5) | (key == spot))
        BIAS[lax.div(i, 2), tile_rows(lax.rem(i, 2), R), :] = jnp.where(
            allowed, 0.0, MASKED
        ).astype(BF)

    loop(TOK // R, roll_tile)
    T3[...] = CT[...].T
    VG[...] = jnp.zeros_like(VG)

    def dy_tile(i):
        VG[7:8, 0:D] += jnp.sum(CT[tile_rows(i, R), :].astype(F32), axis=0, keepdims=True)

    loop(TOK // R, dy_tile)

    if comm:
        for k in z_of["v"]:
            k.wait_recv()

    def spread(row, parts):
        return sum(dot(VPG[z][r : r + 1, :], place_of[p]) for z, r, p in parts)

    place_of = [
        (
            (
                lax.broadcasted_iota(jnp.int32, (256, D), 0) + 192 * p
                == lax.broadcasted_iota(jnp.int32, (256, D), 1)
            )
            & (lax.broadcasted_iota(jnp.int32, (256, D), 0) < 192)
        ).astype(BF)
        for p in range(4)
    ]
    each = lambda r: [(z, r, z) for z in range(4)]
    gain1, shift1 = spread(0, each(0)), spread(1, each(1))
    bias_q = spread(2, [(0, 2, 0), (0, 3, 1), (1, 2, 2), (1, 3, 3)])
    bias_v = spread(3, [(2, 2, 0), (2, 3, 1), (3, 2, 2), (3, 3, 3)])
    bias_o, gain2, shift2, bias_2 = (spread(r, each(r)) for r in (4, 5, 6, 7))
    bias_1 = [
        jnp.concatenate([VPG[z][8 + j : 9 + j, :].astype(F32) for z in range(4)], axis=1)
        for j in range(3)
    ]

    def ln1_tile(i):
        rows = tile_rows(i, R)
        xhat, _ = norm_parts(TK[rows, :].astype(F32))
        HB[rows, :] = (xhat * gain1 + shift1).astype(BF)

    loop(TOK // R, ln1_tile)
    T1[...] = HB[...].T

    def project(h):
        def tile(i):
            rows = tile_rows(i, R)
            p = dot(HB[rows, :], G[:, h * QW : (h + 1) * QW])
            QS[h][rows, 0:384] = ((p[:, 0:384] + bias_q[:, h * 384 : (h + 1) * 384]).astype(BF) * 0.125).astype(BF)
            QS[h][rows, 384:768] = p[:, 384:768].astype(BF)
            QS[h][rows, 768:QW] = (p[:, 768:QW] + bias_v[:, h * 384 : (h + 1) * 384]).astype(BF)

        loop(TOK // R, tile)

    lane = lax.broadcasted_iota(jnp.int32, (1, 128), 1)
    sides = [lane < 64, lane >= 64]

    def forward_pair(h, p, half):
        rows = slice(half * HALF, (half + 1) * HALF)
        q = QS[h][rows, lanes_at(p * 128, 128)]
        k = QS[h][rows, lanes_at(384 + p * 128, 128)]
        v = QS[h][rows, lanes_at(768 + p * 128, 128)]
        vt = v.T
        outs = []
        for e in range(2):
            qe = jnp.where(sides[e], q, 0).astype(BF)
            s = dot_nt(k, qe) + BIAS[half].astype(F32)
            top = jnp.max(s, axis=0, keepdims=True)
            w = jnp.exp(s - top)
            total = jnp.sum(w, axis=0, keepdims=True)
            outs.append(dot(vt[e * 64 : (e + 1) * 64], w.astype(BF)) * (1.0 / total))
            LSE[h * 6 + 2 * p + e, :, rows] = top + jnp.log(total)
        O[rows, lanes_at(h * 384 + p * 128, 128)] = jnp.concatenate(outs, axis=0).astype(BF).T

    def backward_pair(h, p, half):
        rows = slice(half * HALF, (half + 1) * HALF)
        at_q, at_k, at_v = (lanes_at(b + p * 128, 128) for b in (0, 384, 768))
        q, k, v = QS[h][rows, at_q], QS[h][rows, at_k], QS[h][rows, at_v]
        do = H[rows, lanes_at(h * 384 + p * 128, 128)]
        kt = k.T
        dqs, dks, dvs = [], [], []
        for e in range(2):
            qe = jnp.where(sides[e], q, 0).astype(BF)
            de = jnp.where(sides[e], do, 0).astype(BF)
            s = dot_nt(k, qe) + BIAS[half].astype(F32)
            w = jnp.exp(s - LSE[h * 6 + 2 * p + e, :, rows])
            dp = dot_nt(v, de)
            delta = jnp.sum(w * dp, axis=0, keepdims=True)
            ds = (w * (dp - delta)).astype(BF)
            dqs.append(dot(kt[e * 64 : (e + 1) * 64], ds) * 0.125)
            dks.append(dot(ds, q))
            dvs.append(dot(w.astype(BF), do))
        QS[h][rows, at_q] = jnp.concatenate(dqs, axis=0).astype(BF).T
        QS[h][rows, at_k] = jnp.where(sides[0], dks[0], dks[1]).astype(BF)
        QS[h][rows, at_v] = jnp.where(sides[0], dvs[0], dvs[1]).astype(BF)

    def pairs(h, f):
        def body(p):
            for half in range(2):
                f(h, p, half)

        loop(3, body)

    if comm:
        order = [
            on(step_xy, "a"),
            on(step_xy, "b"),
            on(send_z, "o"),
            on(step_diag, "a"),
            on(step_diag, "b"),
            on(send_z, 0),
            on(step_xy, "o"),
            on(step_sib, "a"),
            on(step_sib, "b"),
            on(step_done, "a"),
        ]
        todo += order
        serve(len(order))
    else:
        g_copy.wait()
    project(0)
    if comm:
        todo += [
            on(step_diag, "o"),
            on(step_xy, 0),
            on(step_done, "b"),
            on(send_z, 1),
        ]
        serve(4)
    project(1)
    for h in range(2):
        def body(p):
            for half in range(2):
                forward_pair(h, p, half)

        if comm:
            stages = {
                0: [on(step_sib, "o"), on(step_diag, 0), on(step_xy, 1), on(send_z, 2)],
                1: [on(step_sib, 0), on(step_diag, 1), on(step_done, "o"), on(step_xy, 2)],
            }[h]
            loop(3, body)
            for f in stages:
                f()
        else:
            loop(3, body)

    def mix_tile(i):
        rows = tile_rows(i, R)
        x2 = TK[rows, :].astype(F32) + dot(O[rows, :], G[:, 2 * QW : FC0]) + bias_o
        X2[rows, :] = x2
        xhat, _ = norm_parts(x2)
        HB[rows, :] = (xhat * gain2 + shift2).astype(BF)

    loop(TOK // R, mix_tile)
    T2[...] = HB[...].T

    def feed(j):
        b1, b2 = FC0 + j * FCW, FC0 + j * FCW + 1024
        W1 = lambda: G[:, b1 : b1 + 1024]
        W2 = lambda: G[:, b2 : b2 + 1024]

        def tile(i):
            rows = tile_rows(i, 512)
            a = dot(HB[rows, :], W1()) + bias_1[j]
            act, slope = gelu_parts(a)
            hid = act.astype(BF)
            H[rows, :] = hid
            da = (dot(CT[rows, :], W2()) * slope).astype(BF)
            DA[rows, :] = da
            VG[8 + j : 9 + j, :] += jnp.sum(da.astype(F32), axis=0, keepdims=True)
            up = dot_nt(hid, W2())
            back = dot_nt(da, W1())
            if j == 0:
                YA[rows, :] = up
                DH[rows, :] = back
            else:
                YA[rows, :] += up
                DH[rows, :] += back

        loop(TOK // 512, tile)

    def feed_grads(j):
        b1, b2 = FC0 + j * FCW, FC0 + j * FCW + 1024

        def grads(i):
            rows = tile_rows(i, 256)
            G[rows, b1 : b1 + 1024] = dot(T2[rows, :], DA[...]).astype(BF)
            G[rows, b2 : b2 + 1024] = dot(T3[rows, :], H[...]).astype(BF)

        loop(D // 256, grads)

    if comm:
        seg = {
            0: (G, FC0, FCW), 1: (G, FC0 + FCW, FCW), 2: (G, FC0 + 2 * FCW, FCW),
            "o": (DA, 0, D), "a": (G, FC0, QW), "b": (G, FC0 + FCW, QW),
        }
        slot = {0: 0, 1: FCW, 2: 2 * FCW, "o": 3 * FCW, "a": 0, "b": FCW}
        zslot = {0: 0, 1: 512, 2: 1024, "o": 1536, "a": 1792, "b": 2176}
        rs = {}

        def z_starts(name, z):
            if name == "o":
                return [(128 * (z + lax.div(z, 2)), 256)]
            if name == "a":
                return [(384 * z - 384 * lax.div(z, 3), 384)]
            if name == "b":
                return [(384 * (z - 1) + 384 * lax.div(3 - z, 3), 384)]
            return [(256 * z, 256), (1024 + 256 * z, 256)]

        def mem(name, block, half=None):
            ref, at, width = seg[name]
            at, width = piece(at, width, half)
            return ref.at[rows_of(block), pl.ds(at, width)]

        def red_sib(name):
            width = seg[name][2]
            rs[name] = [
                copies.start(
                    mem(name, 2 * i + 1 - core),
                    RS.at[pl.ds(96 * i, 96), pl.ds(slot[name], width)],
                    (cs, m),
                )
                for i in range(4)
            ]

        def red_diag(name):
            width = seg[name][2]
            for k in rs[name]:
                k.wait_recv()

            def add(i):
                block = mem(name, 2 * i + core)
                block[...] = (
                    block[...].astype(F32)
                    + RS[pl.ds(pl.multiple_of(96 * i, 96), 96), slot[name] : slot[name] + width].astype(F32)
                ).astype(BF)

            loop(4, add)
            rs[name] = [
                copies.start(mem(name, cd, 0), RD.at[:, pl.ds(*piece(slot[name], width, 0))], (cx, m)),
                copies.start(mem(name, cd, 1), RD.at[:, pl.ds(*piece(slot[name], width, 1))], (cy, m)),
            ]

        def red_xy(name):
            width = seg[name][2]
            kx, ky = rs[name]
            kx.wait_recv()
            t = mem(name, cy, 0)
            t[...] = (t[...].astype(F32) + RD[:, pl.ds(*piece(slot[name], width, 0))].astype(F32)).astype(BF)
            ky.wait_recv()
            t = mem(name, cx, 1)
            t[...] = (t[...].astype(F32) + RD[:, pl.ds(*piece(slot[name], width, 1))].astype(F32)).astype(BF)
            at = pl.ds(slot[name], width)
            rs[name] = [
                copies.start(mem(name, cx), RX.at[:, at], (cx, m)),
                copies.start(mem(name, cy), RY.at[:, at], (cy, m)),
            ]

        def red_z(name):
            ref, lo, width = seg[name]
            at = pl.ds(slot[name], width)
            for k in rs[name]:
                k.wait_recv()
            t = mem(name, c)
            t[...] = (t[...].astype(F32) + RX[:, at].astype(F32) + RY[:, at].astype(F32)).astype(BF)
            out = []
            for d, z in enumerate(zs):
                place = zslot[name]
                for s, w in z_starts(name, z):
                    out.append(
                        copies.start(
                            ref.at[rows_of(c), lanes_at(lo + s, w)],
                            RZ.at[d, :, pl.ds(place, w)],
                            (c, z),
                        )
                    )
                    place += w
            rs[name] = out

        def red_end(name):
            for k in rs[name]:
                k.wait_recv()
            ref, lo, width = seg[name]
            place = zslot[name]
            outs = {
                "o": [(go_out, 0)], "a": [(gq_out, 0)], "b": [(gq_out, 384)],
                0: [(g1_out, 0), (g2_out, 0)], 1: [(g1_out, 256), (g2_out, 256)], 2: [(g1_out, 512), (g2_out, 512)],
            }[name]
            for (s, w), (out, col) in zip(z_starts(name, m), outs):
                total = ref[rows_of(c), lanes_at(lo + s, w)].astype(F32)
                for d in range(3):
                    total = total + RZ[d, :, place : place + w].astype(F32)
                out[:, col : col + w] = total
                place += w

    if comm:
        on(step_done, 0)()
        on(step_sib, 1)()
        on(step_diag, 2)()
    feed(0)
    if comm:
        step_done(1)
        step_sib(2)
        copies.drain()
    feed_grads(0)
    if comm:
        red_sib(0)
    feed(1)
    if comm:
        step_done(2)
        red_diag(0)
        red_xy(0)
    feed_grads(1)
    if comm:
        red_sib(1)
        red_z(0)
    feed(2)
    if comm:
        red_diag(1)
        red_xy(1)
        copies.drain()
    feed_grads(2)
    if comm:
        red_sib(2)
        red_end(0)

    def end_tile(i):
        rows = tile_rows(i, R)
        x2 = X2[rows, :]
        HB[rows, :] = (x2 + YA[rows, :] + bias_2).astype(BF)
        xhat, r = norm_parts(x2)
        dh = DH[rows, :]
        VG[5:6, 0:D] += jnp.sum(dh * xhat, axis=0, keepdims=True)
        VG[6:7, 0:D] += jnp.sum(dh, axis=0, keepdims=True)
        dx2 = CT[rows, :].astype(F32) + norm_back(dh, xhat, r, gain2)
        DH[rows, :] = dx2
        dz = dx2.astype(BF)
        CT[rows, :] = dz
        VG[4:5, 0:D] += jnp.sum(dz.astype(F32), axis=0, keepdims=True)
        H[rows, 0:D] = dot_nt(dz, G[:, 2 * QW : FC0]).astype(BF)

    loop(TOK // R, end_tile)
    bo_copy = pltpu.make_async_copy(HB, bo_out, lsem.at[0])
    bo_copy.start()
    T2[...] = O[...].T
    if not comm:
        fc_copy = pltpu.make_async_copy(G.at[:, pl.ds(FC0, 3 * FCW)], dg_out.at[:, pl.ds(FC0, 3 * FCW)], lsem.at[2])
        fc_copy.start()
        fc_copy.wait()

    def out_grads(i):
        rows = tile_rows(i, 256)
        DA[rows, 0:D] = dot(T2[rows, :], CT[...]).astype(BF)

    loop(D // 256, out_grads)
    if comm:
        red_sib("o")
        red_z(1)
        red_diag(2)

    def qkv_grads(h, place):
        def grads(i):
            rows = tile_rows(i, 256)
            G[rows, place : place + QW] = dot(T1[rows, :], QS[h][...]).astype(BF)

        loop(D // 256, grads)
        def sums(i):
            rows = tile_rows(i, R)
            VG[2:3, h * 384 : (h + 1) * 384] += jnp.sum(QS[h][rows, 0:384].astype(F32), axis=0, keepdims=True)
            VG[3:4, h * 384 : (h + 1) * 384] += jnp.sum(QS[h][rows, 768:QW].astype(F32), axis=0, keepdims=True)

        loop(TOK // R, sums)

    pairs(0, backward_pair)
    if comm:
        red_diag("o")
        red_xy(2)
        red_end(1)
        copies.drain()
    qkv_grads(0, FC0)
    if comm:
        red_sib("a")
        red_xy("o")
    pairs(1, backward_pair)
    if comm:
        red_diag("a")
        red_z(2)
        red_z("o")
        copies.drain()
    qkv_grads(1, FC0 + FCW)
    if comm:
        red_sib("b")
        red_xy("a")

    def last_tile(i):
        rows = tile_rows(i, R)
        dh = dot_nt(QA[rows, :], G[:, 0:QW]) + dot_nt(QB[rows, :], G[:, QW : 2 * QW])
        xhat, r = norm_parts(TK[rows, :].astype(F32))
        VG[0:1, 0:D] += jnp.sum(dh * xhat, axis=0, keepdims=True)
        VG[1:2, 0:D] += jnp.sum(dh, axis=0, keepdims=True)
        YA[rows, :] = DH[rows, :] + norm_back(dh, xhat, r, gain1)

    loop(TOK // R, last_tile)
    ig_copy = pltpu.make_async_copy(YA, ig_out, lsem.at[1])
    ig_copy.start()

    if comm:
        vs = copies.start(VG, VR.at[0], (cs, m))
        red_diag("b")
        red_end(2)
        red_end("o")
        vs.wait_recv()
        VB[0] = VG[...] + VR[0]
        vs = copies.start(VB.at[0], VR.at[1], (cx, m))
        red_z("a")
        red_xy("b")
        vs.wait_recv()
        VB[1] = VB[0] + VR[1]
        vs = copies.start(VB.at[1], VR.at[2], (cy, m))
        vs.wait_recv()
        VB[2] = VB[1] + VR[2]
        vs = [copies.start(VB.at[2], VR.at[3 + d], (c, z)) for d, z in enumerate(zs)]
        red_end("a")
        red_z("b")
        for k in vs:
            k.wait_recv()
        vg_out[...] = VB[2] + VR[3] + VR[4] + VR[5]
        red_end("b")
        copies.drain()
    else:
        vg_out[...] = VG[...]
        last = [
            pltpu.make_async_copy(G.at[:, pl.ds(FC0, QW)], dg_out.at[:, pl.ds(0, QW)], lsem.at[2]),
            pltpu.make_async_copy(G.at[:, pl.ds(FC0 + FCW, QW)], dg_out.at[:, pl.ds(QW, QW)], lsem.at[3]),
            pltpu.make_async_copy(DA.at[pl.ds(0, D), pl.ds(0, D)], dg_out.at[:, pl.ds(2 * QW, D)], lsem.at[4]),
        ]
        for k in last:
            k.start()
        for k in last:
            k.wait()
    bo_copy.wait()
    ig_copy.wait()


def run_mega(comm, lens, tok, cot, vis, *rest):
    vm = pl.BlockSpec(memory_space=pltpu.VMEM)
    hbm = pl.BlockSpec(memory_space=pl.ANY)
    smem = pl.BlockSpec(memory_space=pltpu.SMEM)
    S = jax.ShapeDtypeStruct
    outs = [S((TOK, D), BF), S((TOK, D), F32)]
    out_specs = [hbm, hbm]
    if not comm:
        outs += [S((D, COLS), BF), S((16, 1024), F32)]
        out_specs += [hbm, vm]
    else:
        outs += [S((96, D), F32), S((96, 256), F32), S((96, D), F32), S((96, D), F32), S((16, 1024), F32)]
        out_specs += [vm] * 5
    V = pltpu.VMEM
    scratch = [V((D, COLS), BF)]
    scratch += [V((TOK, D), BF), V((TOK, D), BF), V((D, TOK), BF), V((D, TOK), BF), V((D, TOK), BF), V((TOK, D), BF), V((TOK, D), BF)]
    scratch += [V((TOK, QW), BF), V((TOK, QW), BF), V((TOK, D), F32), V((TOK, D), F32), V((TOK, D), F32)]
    scratch += [V((TOK, 1024), BF), V((TOK, 1024), BF), V((2, HALF, HALF), BF), V((HEADS, 1, TOK), F32), V((16, 1024), F32), V((4, 16, 256), BF)]
    scratch += [pltpu.SemaphoreType.DMA((5,))]
    if comm:
        scratch += [V((4, 96, 384), BF), V((4, 96, 384), BF), V((4, 96, 256), BF), V((96, 2 * D), BF)]
        scratch += [V((384, BACK), BF), V((96, BACK), BF), V((96, BACK), BF), V((96, BACK), BF), V((3, 96, 2560), BF)]
        scratch += [V((3, 16, 1024), F32), V((6, 16, 1024), F32), pltpu.SemaphoreType.DMA((160,)), pltpu.SemaphoreType.DMA((160,))]
    return pl.pallas_call(
        functools.partial(mega, comm),
        out_shape=outs,
        in_specs=[smem, hbm, hbm, vm] + ([vm] * 5 if comm else [hbm, vm]),
        out_specs=out_specs,
        scratch_shapes=scratch,
        compiler_params=pltpu.CompilerParams(
            collective_id=0 if comm else None, has_side_effects=comm, vmem_limit_bytes=64 * 2**20
        ),
        cost_estimate=pl.CostEstimate(flops=60 * 10**9, bytes_accessed=20 * 10**6, transcendentals=10**7),
        name="block",
    )(lens, tok, cot, vis, *rest)


def finish(lens, bo_in, ig_in, gq_in, go_in, g2_in, vg_in, bo, ig, gg1, gs1, gq, gbqv, go, gbo, gg2, gs2, gb1, g2, gb2):
    m = lax.axis_index("mlp")
    start, _ = longest_start(lens)

    def tile(i):
        at = lanes_at(i * 128, 128)
        bo[:, at] = pltpu.roll(bo_in[:, at].astype(F32), start, 0).astype(BF)
        ig[:, at] = pltpu.roll(ig_in[:, at], start, 0)

    loop(D // 128, tile)

    def pick(options):
        return jnp.where(m == 0, options[0], jnp.where(m == 1, options[1], jnp.where(m == 2, options[2], options[3])))

    x = gq_in[...]
    a, b = x[:, 0:384], x[:, 384:768]
    cat = lambda p, q: jnp.concatenate([p, q], axis=1)
    gq[...] = pick([cat(a, b[:, 0:192]), cat(b[:, 192:384], a), cat(b, a[:, 0:192]), cat(a[:, 192:384], b)])
    y = go_in[...]
    go[...] = jnp.where(lax.rem(m, 2) == 0, y[:, 0:192], y[:, 64:256])
    g2[...] = g2_in[...].T
    v = vg_in[...]
    row = lambda r: pick([v[r : r + 1, 192 * z : 192 * (z + 1)] for z in range(4)])
    for ref, r in ((gg1, 0), (gs1, 1), (gbo, 4), (gg2, 5), (gs2, 6), (gb2, 7)):
        ref[...] = row(r)
    gbqv[...] = pick([v[2:3, 0:384], v[2:3, 384:768], v[3:4, 0:384], v[3:4, 384:768]])
    gb1[...] = jnp.concatenate(
        [pick([v[8 + j : 9 + j, 256 * z : 256 * (z + 1)] for z in range(4)]) for j in range(3)], axis=1
    )


def run_finish(n, lens, bo, ig, gq, go, g2, vg):
    vm = pl.BlockSpec(memory_space=pltpu.VMEM)
    S = jax.ShapeDtypeStruct
    f = lambda *s: S(s, F32)
    outs = [S((TOK, D), BF), f(TOK, D), f(1, 192), f(1, 192), f(n, 576), f(1, 384), f(n, 192), f(1, 192), f(1, 192), f(1, 192), f(1, 768), f(D, n), f(1, 192)]
    return pl.pallas_call(
        finish,
        out_shape=outs,
        in_specs=[pl.BlockSpec(memory_space=pltpu.SMEM)] + [vm] * 6,
        out_specs=[vm] * len(outs),
        compiler_params=pltpu.CompilerParams(vmem_limit_bytes=48 * 2**20),
        name="finish",
    )(lens, bo, ig, gq, go, g2, vg)


def body_by_collectives(tokens, clip_lengths, vis, vp, w_qkv, w_out, w_fc1, w_fc2, cotangent):
    def whole(x):
        x = lax.all_gather(x, "clips", axis=0, tiled=True)
        return lax.all_gather(x, "mlp", axis=1, tiled=False)

    n, z = w_qkv.shape[0], lax.axis_size("mlp")
    sub = w_fc1.shape[1] // 3
    q = whole(w_qkv).reshape(D, 3, 2, 384).transpose(0, 2, 1, 3).reshape(D, 2 * QW)
    o = whole(w_out).reshape(D, D)
    f = [whole(w).reshape(D, z, 3, sub).transpose(0, 2, 1, 3) for w in (w_fc1, w_fc2.T)]
    g = jnp.concatenate([q, o, jnp.stack(f, axis=2).reshape(D, 3 * FCW)], axis=1)
    vpg = lax.all_gather(vp, "mlp", axis=0, tiled=False)
    bo, ig, dg, vg = run_mega(False, clip_lengths, tokens, cotangent, vis, g, vpg)
    dg = lax.psum_scatter(dg.astype(F32), "clips", scatter_dimension=0, tiled=True)
    dq = dg[:, : 2 * QW].reshape(n, 2, 3, 384).transpose(0, 2, 1, 3).reshape(n, z, -1)
    do = dg[:, 2 * QW : FC0].reshape(n, z, -1)
    df = dg[:, FC0:].reshape(n, 3, 2, z, sub).transpose(2, 0, 3, 1, 4).reshape(2, n, z, -1)
    cut = lambda x: lax.psum_scatter(x, "mlp", scatter_dimension=1, tiled=False)
    vg = lax.psum(vg, ("clips", "mlp"))
    m = lax.axis_index("mlp")
    part = lambda x: lax.dynamic_slice_in_dim(x, m * (x.shape[0] // z), x.shape[0] // z)
    row = lambda r: part(vg[r, :D])
    gb1 = part(vg[8:11].reshape(3, z, sub).transpose(1, 0, 2).reshape(-1))
    start, _ = longest_start(clip_lengths)
    return (
        jnp.roll(bo, start, axis=0), jnp.roll(ig, start, axis=0), row(0), row(1), cut(dq),
        part(vg[2:4, :D].reshape(-1)), cut(do), row(4), row(5), row(6), cut(df[0]), gb1, cut(df[1]).T, row(7),
    )


def body(tokens, clip_lengths, visible, ln1_gain, ln1_bias, w_qkv, b_qv, w_out, b_out, ln2_gain, ln2_bias, w_fc1, b_fc1, w_fc2, b_fc2, cotangent):
    vis = jnp.broadcast_to(visible.reshape(1, TOK), (8, TOK))
    short = jnp.concatenate([ln1_gain, ln1_bias, b_qv, b_out, ln2_gain, ln2_bias, b_fc2]).reshape(8, 192)
    vp = jnp.concatenate([jnp.pad(short, ((0, 0), (0, 64))), b_fc1.reshape(3, 256), jnp.zeros((5, 256), BF)], axis=0)
    clips, mlp = lax.axis_size("clips"), lax.axis_size("mlp")
    if (clips, mlp) != (8, 4):
        return body_by_collectives(
            tokens, clip_lengths, vis, vp, w_qkv, w_out, w_fc1, w_fc2, cotangent
        )
    bo, ig, gq, go, g1, g2, vg = run_mega(True, clip_lengths, tokens, cotangent, vis, w_qkv, w_out, w_fc1, w_fc2, vp)
    bo, ig, gg1, gs1, gq, gbqv, go, gbo, gg2, gs2, gb1, g2, gb2 = run_finish(96, clip_lengths, bo, ig, gq, go, g2, vg)
    flat = lambda x: x.reshape(-1)
    return (bo, ig, flat(gg1), flat(gs1), gq, flat(gbqv), go, flat(gbo), flat(gg2), flat(gs2), g1, flat(gb1), g2, flat(gb2))


def solution(mesh):
    in_specs = (
        P(("clips", "mlp"), None), P(("clips", "mlp"), None), P(("clips", "mlp")), P("mlp"), P("mlp"),
        P("clips", "mlp"), P("mlp"), P("clips", "mlp"), P("mlp"), P("mlp"), P("mlp"), P("clips", "mlp"),
        P("mlp"), P("mlp", "clips"), P("mlp"), P(("clips", "mlp"), None),
    )
    out_specs = (
        P(("clips", "mlp"), None), P(("clips", "mlp"), None), P("mlp"), P("mlp"), P("clips", "mlp"), P("mlp"),
        P("clips", "mlp"), P("mlp"), P("mlp"), P("mlp"), P("clips", "mlp"), P("mlp"), P("mlp", "clips"), P("mlp"),
    )
    return jax.shard_map(body, mesh=mesh, in_specs=in_specs, out_specs=out_specs, check_vma=False)
```

```python
import functools

import jax
import jax.numpy as jnp
from jax import lax
from jax.experimental import pallas as pl
from jax.experimental.pallas import tpu as pltpu
from jax.sharding import PartitionSpec as P

F32 = jnp.float32
BF = jnp.bfloat16
MESH = pl.DeviceIdType.MESH
HEADS = 12
HEAD_DIM = 64
NORM_EPS = 1e-06
MASKED = -1000000000.0
D = 768
TOK = 1024
HALF = 512
FCW = 2048
PAIRS = (1, 2, 2, 1)
FIRST = (0, 1, 3, 5)
HELD = ((0, 1, 2, None), (0, 1, 2, 2), (0, 0, 1, 2), (None, 0, 1, 2))
WIDTH = {f"q{g}": 384 * n for g, n in enumerate(PAIRS)}
WIDTH.update(o=D, f0=FCW, f1=FCW, f2=FCW)
NAMES = tuple(WIDTH)
COLS = sum(WIDTH.values())
PLACE = {n: sum(list(WIDTH.values())[:i]) for i, n in enumerate(NAMES)}
ZW = {f"q{g}": 128 * n for g, n in enumerate(PAIRS)}
ZW.update(o=256, f0=256, f1=256, f2=256)
SEGS = {n: 2 if n[0] == "f" else 1 for n in NAMES}
ZPLACE = {n: sum(ZW[k] * SEGS[k] for k in NAMES[:i]) for i, n in enumerate(NAMES)}
ZCOLS = sum(ZW[n] * SEGS[n] for n in NAMES)
R = 256
FORWARD = 128
BACKWARD = 256


def dot(a, b):
    return jnp.dot(a, b, preferred_element_type=F32)


def dot_nt(a, b):
    return lax.dot_general(a, b, (((1,), (1,)), ((), ())), preferred_element_type=F32)


def tile_rows(i, size):
    return pl.ds(pl.multiple_of(i * size, size), size)


def lanes_at(start, size):
    return pl.ds(pl.multiple_of(start, 128), size)


def loop(count, body, hooks=None):
    def step(i, carry):
        body(i)
        for k, f in (hooks or {}).items():
            pl.when(i == k)(f)
        return carry

    lax.fori_loop(0, count, step, 0)


def norm_parts(x):
    mean = jnp.mean(x, axis=-1, keepdims=True)
    centred = x - mean
    spread = jnp.mean(centred * centred, axis=-1, keepdims=True)
    r = lax.rsqrt(spread + NORM_EPS)
    return centred * r, r


def norm_back(dh, xhat, r, gain):
    e = dh * gain
    m1 = jnp.mean(e, axis=-1, keepdims=True)
    m2 = jnp.mean(e * xhat, axis=-1, keepdims=True)
    return r * (e - m1 - xhat * m2)


def gelu_parts(a):
    e = jnp.exp(a * a * -0.5)
    t = 1.0 / (1.0 + jnp.abs(a) * (0.3275911 * 0.7071067811865476))
    poly = t * (
        0.254829592
        + t * (-0.284496736 + t * (1.421413741 + t * (-1.453152027 + t * 1.061405429)))
    )
    half = 0.5 * poly * e
    phi = jnp.where(a < 0, half, 1.0 - half)
    return a * phi, phi + a * e * 0.3989422804014327


def longest_start(lens):
    n0, n1, n2, n3 = lens[0, 0], lens[0, 1], lens[0, 2], lens[0, 3]
    top = jnp.maximum(jnp.maximum(n0, n1), jnp.maximum(n2, n3))
    start = jnp.where(
        n0 == top, 0, jnp.where(n1 == top, n0, jnp.where(n2 == top, n0 + n1, n0 + n1 + n2))
    )
    return start, (n0, n0 + n1, n0 + n1 + n2)


def one_hot_cols(rows, cols, shift):
    r = lax.broadcasted_iota(jnp.int32, (rows, cols), 0)
    c = lax.broadcasted_iota(jnp.int32, (rows, cols), 1)
    return (r == c + shift).astype(BF)


class Links:
    def __init__(self, send, recv):
        self.send, self.recv, self.table = send, recv, {}

    def add(self, key, src, dst, device):
        self.table[key] = (len(self.table), src, dst, device)

    def copy(self, key):
        k, src, dst, device = self.table[key]
        return pltpu.make_async_remote_copy(
            src_ref=src(),
            dst_ref=dst(),
            send_sem=self.send.at[k],
            recv_sem=self.recv.at[k],
            device_id=device,
            device_id_type=MESH,
        )

    def start(self, *keys):
        for key in keys:
            self.copy(key).start()

    def got(self, *keys):
        for key in keys:
            self.copy(key).wait_recv()

    def sent(self, *keys):
        for key in keys:
            self.copy(key).wait_send()


def places():
    c = lax.axis_index("clips")
    m = lax.axis_index("mlp")
    core = lax.rem(c, 2)
    x = lax.rem(lax.div(c, 2), 2)
    y = lax.div(c, 4)
    cs = c + 1 - 2 * core
    cx = c + 2 - 4 * x
    cy = c + 4 - 8 * y
    cd = cx + 4 - 8 * y
    zs = [lax.rem(m + d, 4) for d in (1, 2, 3)]
    return c, m, core, cs, cx, cy, cd, zs


def rows_of(c):
    return pl.ds(pl.multiple_of(c * 96, 16), 96)


def rooms(refs):
    out = {f"f{j}": ref for j, ref in enumerate(refs)}
    for n, j, at in (("o", 0, 0), ("q0", 0, 768), ("q1", 0, 1152), ("q2", 1, 0), ("q3", 1, 768)):
        out[n] = refs[j].at[:, pl.ds(at, WIDTH[n])]
    return out


def half_rows_of(c, half):
    return pl.ds(pl.multiple_of(c * 96 + 48 * half, 16), 48)


def by_device(m, values):
    out = values[3]
    for z in (2, 1, 0):
        out = jnp.where(m == z, values[z], out)
    return out


def pack_vectors(vectors):
    gain1, shift1, b_qv, b_o, gain2, shift2, b_2, b_1 = (v.astype(F32).reshape(1, -1) for v in vectors)
    pad = lambda v: jnp.concatenate([v, jnp.zeros((1, 64), F32)], axis=1)
    rows = [pad(v) for v in (gain1, shift1, b_qv[:, 0:192], b_qv[:, 192:384], b_o, gain2, shift2, b_2)]
    rows += [b_1[:, 256 * j : 256 * (j + 1)] for j in range(3)]
    line = lax.broadcasted_iota(jnp.int32, (16, 256), 0)
    out = jnp.zeros((16, 256), F32)
    for r, v in enumerate(rows):
        out = jnp.where(line == r, v, out)
    return out.astype(BF)


GZ, GM, GX, GY, GS, GF, RS, RD, RA, RB, RZ, RE, EARLY, LATE = range(14)
Q0, Q1, Q2, Q3, OUT, F0, F1, F2 = range(8)
START, PACK, ROLL, VEC, LN, T1, DY, NEED, PROJECT, FWD, MIX, T2, T3, FEED, FG, DONE, END, OT, OG, BWD, DHP, QG, LAST = range(23)
SCHEDULE = {
    (START,): ((GZ, Q1), (GZ, Q2), (GZ, OUT),),
    (ROLL, 2): ((GM, Q0),),
    (LN, 3): ((GM, Q1),),
    (DY,): ((GX, Q0), (GY, Q0), (GZ, Q3), (GZ, F0), (GZ, F1),),
    (NEED, Q0): ((GM, Q2), (GX, Q1), (GY, Q1), (GS, Q0), (GM, OUT), (GM, Q3), (GX, Q2), (GY, Q2), (GF, Q0),),
    (FWD, 0, 0): ((GS, Q1),),
    (NEED, Q1): ((GX, OUT), (GY, OUT), (GX, Q3), (GF, Q1), (GY, Q3),),
    (PROJECT, 1): ((GS, Q2), (GM, F0), (GZ, F2),),
    (FWD, 1, 0): ((GS, OUT),),
    (FWD, 1, 1): ((GS, Q3),),
    (FWD, 1, 2): ((GF, Q2),),
    (FWD, 1, 3): ((GF, OUT),),
    (PROJECT, 2): ((GF, Q3), (GM, F1),),
    (FWD, 2, 2): ((GX, F0), (GY, F0),),
    (T3,): ((GX, F1), (GY, F1), (GM, F2),),
    (NEED, F0): ((GS, F0), (GS, F1), (GF, F0),),
    (FEED, 0, 0): ((GF, F1),),
    (FEED, 0, 1): ((GX, F2), (GY, F2),),
    (DONE, F0): ((RS, F0),),
    (FEED, 1, 0): ((GS, F2),),
    (FEED, 1, 1): ((RD, F0),),
    (FG, 1, 0): ((GF, F2),),
    (DONE, F1): ((RS, F1),),
    (FEED, 2, 0): ((RA, F0), (RB, F0),),
    (FEED, 2, 1): ((RD, F1),),
    (DONE, F2): ((RS, F2),),
    (END, 2): ((RZ, F0),),
    (END, 3): ((RD, F2),),
    (OG, 1): ((RA, F1), (RB, F1),),
    (DONE, OUT): ((RS, OUT),),
    (DONE, END): ((EARLY, 0),),
    (DHP, 0): ((RA, F2), (RB, F2), (RD, OUT), (EARLY, 1),),
    (QG, 0): ((RE, F0),),
    (DONE, Q0): ((RS, Q0),),
    (BWD, 1, 1): ((RD, Q0),),
    (BWD, 1, 2): ((RZ, F1),),
    (QG, 1): ((RZ, F2),),
    (DONE, Q1): ((RS, Q1),),
    (BWD, 2, 0): ((RA, OUT), (RB, OUT), (RB, Q0), (EARLY, 2),),
    (BWD, 2, 1): ((RE, F1), (RA, Q0), (RD, Q1),),
    (BWD, 2, 3): ((RZ, OUT), (EARLY, 3),),
    (DHP, 2): ((RZ, Q0), (RA, Q1),),
    (QG, 2): ((RE, F2), (RB, Q1),),
    (DONE, Q2): ((RS, Q2),),
    (BWD, 3, 0): ((RE, OUT),),
    (QG, 3): ((RD, Q2), (RZ, Q1),),
    (DONE, Q3): ((RS, Q3),),
    (LAST, 0): ((EARLY, 4),),
    (LAST, 1): ((RE, Q0),),
    (LAST, 3): ((RA, Q2), (RB, Q2), (RD, Q3),),
    (DONE, LAST): ((LATE, 0),),
    (NEED, LAST): ((RE, Q1), (LATE, 1), (RZ, Q2), (RB, Q3), (RA, Q3), (LATE, 2), (RZ, Q3), (LATE, 3), (RE, Q2), (RE, Q3), (LATE, 4),),
}


def mega(comm, *refs):
    refs = list(refs)

    def take(n):
        out = refs[:n]
        del refs[:n]
        return out

    lens, tok_in, cot_in, vis = take(4)
    if comm:
        wq_in, wo_in, w1_in, w2_in = take(4)
        vec_in = take(8)
    else:
        g_in, vpg_in = take(2)
    bo_out, ig_out = take(2)
    if comm:
        gq_out, go_out, g1_out, g2_out, vg_out, vl_out = take(6)
    else:
        dg_out, vg_out, vl_out = take(3)
    G = dict(zip(NAMES, take(8)))
    TK, CT, H1T, H2T, DYT, HB, O = take(7)
    QS = take(4)
    YA, DH, H, DA, BIAS, LSE, VG, VL, VPG, lsem = take(10)
    if comm:
        Z = dict(zip(NAMES[:5], take(5)))
        SB, DB, XB, YB = (rooms(take(3)) for _ in range(4))
        ZB, VB, VR, UB, UR, ssem, rsem = take(7)

    tok_copy = pltpu.make_async_copy(tok_in, H.at[:, pl.ds(0, D)], lsem.at[0])
    cot_copy = pltpu.make_async_copy(cot_in, DA.at[:, pl.ds(0, D)], lsem.at[1])
    bo_copy = pltpu.make_async_copy(HB, bo_out, lsem.at[0])
    ig_copy = pltpu.make_async_copy(YA, ig_out, lsem.at[1])
    tok_copy.start()
    cot_copy.start()

    if comm:
        c, m, core, cs, cx, cy, cd, zs = places()
        links = Links(ssem, rsem)
        to_s, to_x, to_y, to_z = (cs, m), (cx, m), (cy, m), [(c, z) for z in zs]
        barrier = pltpu.get_barrier_semaphore()
        for p in [to_s, to_x, to_y] + to_z:
            pl.semaphore_signal(barrier, inc=1, device_id=p, device_id_type=MESH)

        def mine():
            return rows_of(c)

        def part(n, block, half=None):
            return lambda: G[n].at[rows_of(block) if half is None else half_rows_of(block, half)]

        def both(key, ref, device):
            links.add(key, ref, ref, device)

        def z_seg(n, s):
            if n[0] != "f":
                return lambda: Z[n].at[m]
            return lambda: G[n].at[mine(), lanes_at(s * 1024 + m * 256, 256)]

        z_keys, n_keys = {}, {}
        for n in NAMES:
            z_keys[n] = [("z", n, s, d) for s in range(SEGS[n]) for d in range(3)]
            for _, _, s, d in z_keys[n]:
                both(("z", n, s, d), z_seg(n, s), to_z[d])
            both(("x", n), part(n, c), to_x)
            both(("y", n), part(n, c), to_y)
            both(("dy", n), part(n, cx, 0), to_y)
            both(("dx", n), part(n, cy, 1), to_x)
            for i, block in enumerate((c, cx, cy, cd)):
                both((f"s{i}", n), part(n, block), to_s)
            n_keys[n] = [(k, n) for k in ("x", "y", "dy", "dx", "s0", "s1", "s2", "s3")]
        for d in range(3):
            both(("v", d), lambda: VPG.at[m], to_z[d])

        def gz(n):
            links.start(*z_keys[n])

        def gm(n):
            links.got(*z_keys[n])
            if n[0] == "q":
                w = ZW[n]
                for t in range(3):
                    G[n][mine(), t * w : (t + 1) * w] = sum(Z[n][z] for z in range(4) if HELD[int(n[1])][z] == t)
            elif n == "o":
                for h in range(2):
                    b, lo, hi = 384 * h, Z[n][2 * h], Z[n][2 * h + 1]
                    G[n][mine(), b : b + 128] = lo[:, 0:128]
                    G[n][mine(), b + 128 : b + 256] = lo[:, 128:256] + hi[:, 0:128]
                    G[n][mine(), b + 256 : b + 384] = hi[:, 128:256]
            links.start(("x", n), ("y", n), ("s0", n))

        def gdx(n):
            links.got(("x", n))
            links.start(("dy", n), ("s1", n))

        def gdy(n):
            links.got(("y", n))
            links.start(("dx", n), ("s2", n))

        def gs(n):
            links.got(("dy", n), ("dx", n))
            links.start(("s3", n))

        def gf(n):
            links.got(*[(f"s{i}", n) for i in range(4)])

        def gone(n):
            links.sent(*z_keys[n], *n_keys[n])

        back = dict(G)
        back["q3"] = DA

        def z_starts(n, z):
            if n == "o":
                return [128 * (z + lax.div(z, 2))]
            if n[0] == "q":
                return [ZW[n] * by_device(z, [t or 0 for t in HELD[int(n[1])]])]
            return [256 * z, 1024 + 256 * z]

        def mem(n, block, half=None):
            rows = lambda: rows_of(block) if half is None else half_rows_of(block, half)
            return lambda: back[n].at[rows(), pl.ds(0, WIDTH[n])]

        def room(ref, n, half=None):
            if half is None:
                return lambda: ref[n]
            return lambda: ref[n].at[pl.ds(48 * half, 48)]

        def z_from(n, s, d):
            return lambda: back[n].at[mine(), lanes_at(z_starts(n, zs[d])[s], ZW[n])]

        def z_room(n, s, d):
            return lambda: ZB.at[d, :, pl.ds(ZPLACE[n] + ZW[n] * s, ZW[n])]

        r_keys = {}
        for n in NAMES:
            for i in range(4):
                links.add(("S", n, i), mem(n, 2 * i + 1 - core), lambda n=n, i=i: SB[n].at[pl.ds(96 * i, 96)], to_s)
            links.add(("DX", n), mem(n, cd, 0), room(DB, n, 0), to_x)
            links.add(("DY", n), mem(n, cd, 1), room(DB, n, 1), to_y)
            links.add(("X", n), mem(n, cx), room(XB, n), to_x)
            links.add(("Y", n), mem(n, cy), room(YB, n), to_y)
            r_keys[n] = [("Z", n, s, d) for s in range(SEGS[n]) for d in range(3)]
            for _, _, s, d in r_keys[n]:
                links.add(("Z", n, s, d), z_from(n, s, d), z_room(n, s, d), to_z[d])

        def rS(n):
            links.start(*[("S", n, i) for i in range(4)])

        def rD(n):
            links.got(*[("S", n, i) for i in range(4)])

            def add(block):
                ref = mem(n, block)()
                other = SB[n][rows_of(lax.div(block, 2)), :]
                ref[...] = (ref[...].astype(F32) + other.astype(F32)).astype(BF)

            add(cd)
            links.start(("DX", n), ("DY", n))
            for block in (cx, cy, c):
                add(block)

        def rXa(n):
            links.got(("DX", n))
            t, u = mem(n, cy, 0)(), room(DB, n, 0)()
            t[...] = (t[...].astype(F32) + u[...].astype(F32)).astype(BF)
            links.start(("Y", n))

        def rXb(n):
            links.got(("DY", n))
            t, u = mem(n, cx, 1)(), room(DB, n, 1)()
            t[...] = (t[...].astype(F32) + u[...].astype(F32)).astype(BF)
            links.start(("X", n))

        def rZ(n):
            links.got(("X", n), ("Y", n))
            t = mem(n, c)()
            t[...] = (
                t[...].astype(F32) + room(XB, n)()[...].astype(F32) + room(YB, n)()[...].astype(F32)
            ).astype(BF)
            links.start(*r_keys[n])

        def rE(n):
            links.got(*r_keys[n])
            k = 128 * FIRST[int(n[1])] if n[0] == "q" else 256 * int(n[1]) if n[0] == "f" else 0
            outs = {"o": [go_out], "q": [gq_out], "f": [g1_out, g2_out]}[n[0]]
            w = ZW[n]
            for s, out in enumerate(outs):
                total = back[n][mine(), lanes_at(z_starts(n, m)[s], w)].astype(F32)
                for d in range(3):
                    total = total + ZB[d, :, ZPLACE[n] + w * s : ZPLACE[n] + w * (s + 1)].astype(F32)
                out[:, k : k + w] = total

        def back_gone(n):
            links.sent(*[("S", n, i) for i in range(4)], ("DX", n), ("DY", n), ("X", n), ("Y", n), *r_keys[n])

        v_keys = {}
        for r, (src, buf, rec) in {"e": (VG, VB, VR), "l": (VL, UB, UR)}.items():
            links.add(r + "0", lambda src=src: src, lambda rec=rec: rec.at[0], to_s)
            links.add(r + "1", lambda buf=buf: buf.at[0], lambda rec=rec: rec.at[1], to_x)
            links.add(r + "2", lambda buf=buf: buf.at[1], lambda rec=rec: rec.at[2], to_y)
            v_keys[r] = [(r + "3", d) for d in range(3)]
            for d in range(3):
                links.add((r + "3", d), lambda buf=buf: buf.at[2], lambda rec=rec, d=d: rec.at[3 + d], to_z[d])

        def rv(r, k):
            src, buf, rec, out = (VG, VB, VR, vg_out) if r == "e" else (VL, UB, UR, vl_out)
            if k in (1, 2, 3):
                links.got(r + str(k - 1))
                buf[k - 1] = (src[...] if k == 1 else buf[k - 2]) + rec[k - 1]
            if k < 3:
                links.start(r + str(k))
            elif k == 3:
                links.start(*v_keys[r])
            else:
                links.got(*v_keys[r])
                out[...] = buf[2] + rec[3] + rec[4] + rec[5]

        wq = wq_in[...]
        def shard(g):
            n = f"q{g}"
            off = [
                768 * HELD[g][z] + 128 * FIRST[g] - 576 * z if HELD[g][z] is not None else -4096
                for z in range(4)
            ]
            Z[n][m] = dot(wq, one_hot_cols(576, ZW[n], by_device(m, off))).astype(BF)

        shard(0)
        VPG[m] = pack_vectors([v[...] for v in vec_in])
        pl.semaphore_wait(barrier, 6)
        gz("q0")
        links.start(*[("v", d) for d in range(3)])
        for g in (1, 2, 3):
            shard(g)
        Z["o"][m] = dot(wo_in[...], one_hot_cols(192, 256, jnp.where(lax.rem(m, 2) == 0, 0, -64))).astype(BF)
        for j in range(3):
            for s, w in enumerate((w1_in, w2_in)):
                G[f"f{j}"][mine(), lanes_at(s * 1024 + m * 256, 256)] = w[:, j * 256 : (j + 1) * 256]
    else:
        g_copies = [
            pltpu.make_async_copy(g_in.at[:, pl.ds(PLACE[n], WIDTH[n])], G[n], lsem.at[2 + i])
            for i, n in enumerate(NAMES)
        ]
        for k in g_copies:
            k.start()
        VPG[...] = vpg_in[...]

    def serve(*label):
        if not comm:
            return
        table = (gz, gm, gdx, gdy, gs, gf, rS, rD, rXa, rXb, rZ, rE)
        for f, n in SCHEDULE.get(label, ()):
            if f in (EARLY, LATE):
                rv("el"[f - EARLY], n)
            else:
                table[f](NAMES[n])

    def leave(n):
        if comm:
            gone(n)

    def served(count, body, *label):
        hooks = {i: functools.partial(serve, *label, i) for i in range(count) if (*label, i) in SCHEDULE}
        loop(count, body, hooks if comm else None)

    start, ends = longest_start(lens)
    tok_copy.wait()
    cot_copy.wait()
    vis8 = jnp.broadcast_to(vis[...], (8, TOK)).astype(F32).astype(BF)

    def roll_tile(i):
        rows = tile_rows(i, R)
        place = lax.broadcasted_iota(jnp.int32, (R, 1), 0) + i * R + start
        place = jnp.where(place >= TOK, place - TOK, place)
        perm = (lax.broadcasted_iota(jnp.int32, (R, TOK), 1) == place).astype(BF)
        TK[rows, :] = dot(perm, H[:, 0:D]).astype(BF)
        CT[rows, :] = dot(perm, DA[:, 0:D]).astype(BF)
        clip = sum((place >= e).astype(jnp.int32) for e in ends)
        spot = lax.broadcasted_iota(jnp.int32, (R, 1), 0) + lax.rem(i, 2) * R
        key = lax.broadcasted_iota(jnp.int32, (1, HALF), 1)
        far = key + lax.div(i, 2) * HALF + start
        far = jnp.where(far >= TOK, far - TOK, far)
        clip_k = sum((far >= e).astype(jnp.int32) for e in ends)
        whole = lax.broadcasted_iota(jnp.int32, (HALF, TOK), 0) + lax.div(i, 2) * HALF + start
        whole = jnp.where(whole >= TOK, whole - TOK, whole)
        keys = (lax.broadcasted_iota(jnp.int32, (HALF, TOK), 1) == whole).astype(BF)
        seen = dot_nt(vis8, keys)[0:1, :]
        allowed = (clip == clip_k) & ((seen > 0.5) | (key == spot))
        BIAS[lax.div(i, 2), tile_rows(lax.rem(i, 2), R), :] = jnp.where(
            allowed, 0.0, MASKED
        ).astype(BF)

    serve(START)
    serve(PACK)
    served(TOK // R, roll_tile, ROLL)

    if comm:
        links.got(*[("v", d) for d in range(3)])

    def spread(parts):
        return sum(dot(VPG[z][r : r + 1, :], place_of[p]) for z, r, p in parts)

    place_of = [
        (
            (
                lax.broadcasted_iota(jnp.int32, (256, D), 0) + 192 * p
                == lax.broadcasted_iota(jnp.int32, (256, D), 1)
            )
            & (lax.broadcasted_iota(jnp.int32, (256, D), 0) < 192)
        ).astype(BF)
        for p in range(4)
    ]
    each = lambda r: [(z, r, z) for z in range(4)]
    gain1, shift1 = spread(each(0)), spread(each(1))
    bias_q = spread([(0, 2, 0), (0, 3, 1), (1, 2, 2), (1, 3, 3)])
    bias_v = spread([(2, 2, 0), (2, 3, 1), (3, 2, 2), (3, 3, 3)])
    bias_o, gain2, shift2, bias_2 = (spread(each(r)) for r in (4, 5, 6, 7))
    bias_1 = [
        jnp.concatenate([VPG[z][8 + j : 9 + j, :].astype(F32) for z in range(4)], axis=1)
        for j in range(3)
    ]

    serve(VEC)

    def ln1_tile(i):
        rows = tile_rows(i, R)
        xhat, _ = norm_parts(TK[rows, :].astype(F32))
        HB[rows, :] = (xhat * gain1 + shift1).astype(BF)

    served(TOK // R, ln1_tile, LN)
    H1T[...] = HB[...].T
    LSE[...] = jnp.zeros_like(LSE)
    serve(T1)
    VG[...] = jnp.zeros_like(VG)
    VL[...] = jnp.zeros_like(VL)

    def dy_tile(i):
        VG[3:4, 0:D] += jnp.sum(CT[tile_rows(i, R), :].astype(F32), axis=0, keepdims=True)

    loop(TOK // R, dy_tile)
    serve(DY)
    if not comm:
        for k in g_copies:
            k.wait()

    def project(g):
        def tile(i):
            rows = tile_rows(i, R)
            p = dot(HB[rows, :], G[f"q{g}"][...])
            w = ZW[f"q{g}"]
            cols = slice(128 * FIRST[g], 128 * FIRST[g] + w)
            QS[g][rows, 0:w] = ((p[:, 0:w] + bias_q[:, cols]).astype(BF) * 0.125).astype(BF)
            QS[g][rows, w : 2 * w] = p[:, w : 2 * w].astype(BF)
            QS[g][rows, 2 * w :] = (p[:, 2 * w :] + bias_v[:, cols]).astype(BF)

        loop(TOK // R, tile)

    lane = lax.broadcasted_iota(jnp.int32, (1, 128), 1)
    sides = [lane < 64, lane >= 64]

    def unit_of(u):
        return lax.div(u, 2), lax.rem(u, 2)

    def two_heads(x):
        return jnp.concatenate([jnp.where(sides[0], x, 0), jnp.where(sides[1], x, 0)], axis=0).astype(BF)

    def twice(x):
        return jnp.concatenate([x, x], axis=0)

    def forward_unit(g):
        def unit(u):
            p, half = unit_of(u)
            rows = tile_rows(half, HALF)
            head = 2 * (FIRST[g] + p)
            k = QS[g][rows, lanes_at(ZW[f"q{g}"] + p * 128, 128)]
            v = QS[g][rows, lanes_at(2 * ZW[f"q{g}"] + p * 128, 128)]
            v1 = jnp.concatenate([v, jnp.ones((HALF, 128), BF)], axis=1)
            for a in range(0, HALF, FORWARD):
                some = pl.ds(pl.multiple_of(half * HALF + a, FORWARD), FORWARD)
                q = QS[g][some, lanes_at(p * 128, 128)]
                s = dot_nt(two_heads(q), k) + twice(BIAS[half, a : a + FORWARD, :].astype(F32))
                top = jnp.max(s, axis=1, keepdims=True)
                out = dot(jnp.exp(s - top).astype(BF), v1)
                even, odd = out[:FORWARD], out[FORWARD:]
                total = jnp.where(sides[0], even[:, 128:], odd[:, 128:])
                O[some, lanes_at((FIRST[g] + p) * 128, 128)] = (
                    jnp.where(sides[0], even[:, :128], odd[:, :128]) / total
                ).astype(BF)
                LSE[some, :] = jnp.where(
                    lane == head,
                    top[:FORWARD] + jnp.log(even[:, 128:]),
                    jnp.where(lane == head + 1, top[FORWARD:] + jnp.log(odd[:, 128:]), LSE[some, :]),
                )

        return unit

    def backward_unit(g):
        def unit(u):
            p, half = unit_of(u)
            rows = tile_rows(half, HALF)
            at_q, at_k, at_v = (lanes_at(b * ZW[f"q{g}"] + p * 128, 128) for b in range(3))
            at_o = lanes_at((FIRST[g] + p) * 128, 128)
            head = 2 * (FIRST[g] + p)
            k, v = QS[g][rows, at_k], QS[g][rows, at_v]
            dk = dv = 0.0
            for a in range(0, HALF, BACKWARD):
                some = pl.ds(pl.multiple_of(half * HALF + a, BACKWARD), BACKWARD)
                q, do = two_heads(QS[g][some, at_q]), two_heads(H[some, at_o])
                both = H[some, at_o].astype(F32) * O[some, at_o].astype(F32)
                pick = lambda which, x: jnp.sum(jnp.where(which, x, 0.0), axis=1, keepdims=True)
                delta = jnp.concatenate([pick(sides[0], both), pick(sides[1], both)], axis=0)
                lse = LSE[some, :]
                lse = jnp.concatenate([pick(lane == head, lse), pick(lane == head + 1, lse)], axis=0)
                s = dot_nt(q, k) + twice(BIAS[half, a : a + BACKWARD, :].astype(F32))
                w = jnp.exp(s - lse)
                ds = (w * (dot_nt(do, v) - delta)).astype(BF)
                w = w.astype(BF)
                dq = dot(ds, k)
                QS[g][some, at_q] = (jnp.where(sides[0], dq[:BACKWARD], dq[BACKWARD:]) * 0.125).astype(BF)
                dk = dk + dot(q.T, ds)
                dv = dv + dot(do.T, w)
            QS[g][rows, at_k] = dk.astype(BF).T
            QS[g][rows, at_v] = dv.astype(BF).T

        return unit

    for g in range(4):
        serve(NEED, Q0 + g)
        project(g)
        serve(PROJECT, g)
        served(2 * PAIRS[g], forward_unit(g), FWD, g)
    serve(NEED, OUT)

    def mixed(rows):
        return TK[rows, :].astype(F32) + dot(O[rows, :], G["o"][...]) + bias_o

    def mix_tile(i):
        rows = tile_rows(i, R)
        x2 = mixed(rows)
        xhat, _ = norm_parts(x2)
        HB[rows, :] = (xhat * gain2 + shift2).astype(BF)

    served(TOK // R, mix_tile, MIX)
    H2T[...] = HB[...].T
    serve(T2)
    DYT[...] = CT[...].T
    serve(T3)

    def feed(j):
        W1 = lambda: G[f"f{j}"][:, 0:1024]
        W2 = lambda: G[f"f{j}"][:, 1024:]
        act, slope = gelu_parts(dot(HB[...], W1()) + bias_1[j])
        H[...] = act.astype(BF)
        da = (dot(CT[...], W2()) * slope).astype(BF)
        DA[...] = da
        VG[4 + j : 5 + j, :] += jnp.sum(da.astype(F32), axis=0, keepdims=True)
        serve(FEED, j, 0)
        if j == 0:
            YA[...] = dot_nt(H[...], W2())
            DH[...] = dot_nt(DA[...], W1())
        else:
            YA[...] += dot_nt(H[...], W2())
            DH[...] += dot_nt(DA[...], W1())
        serve(FEED, j, 1)

    def feed_grads(j):
        G[f"f{j}"][:, 0:1024] = dot(H2T[...], DA[...]).astype(BF)
        G[f"f{j}"][:, 1024:] = dot(DYT[...], H[...]).astype(BF)

    for j in range(3):
        serve(NEED, F0 + j)
        feed(j)
        leave(f"f{j}")
        feed_grads(j)
        serve(FG, j, 0)
        serve(DONE, F0 + j)

    def end_tile(i):
        rows = tile_rows(i, R)
        x2 = mixed(rows)
        HB[rows, :] = (x2 + YA[rows, :] + bias_2).astype(BF)
        xhat, r = norm_parts(x2)
        dh = DH[rows, :]
        VG[1:2, 0:D] += jnp.sum(dh * xhat, axis=0, keepdims=True)
        VG[2:3, 0:D] += jnp.sum(dh, axis=0, keepdims=True)
        dx2 = CT[rows, :].astype(F32) + norm_back(dh, xhat, r, gain2)
        DH[rows, :] = dx2
        dz = dx2.astype(BF)
        CT[rows, :] = dz
        VG[0:1, 0:D] += jnp.sum(dz.astype(F32), axis=0, keepdims=True)
        H[rows, 0:D] = dot_nt(dz, G["o"][...]).astype(BF)

    served(TOK // R, end_tile, END)
    bo_copy.start()
    H2T[...] = O[...].T
    serve(OT)
    leave("o")

    def out_grads(i):
        rows = tile_rows(i, 256)
        G["o"][rows, :] = dot(H2T[rows, :], CT[...]).astype(BF)

    served(D // 256, out_grads, OG)
    serve(DONE, OUT)
    serve(DONE, END)

    def dh1_part(g, rows):
        return dot_nt(QS[g][rows, :], G[f"q{g}"][...])

    def dh1_tile(g):
        def tile(i):
            rows = tile_rows(i, R)
            if g == 0:
                YA[rows, :] = dh1_part(g, rows)
            else:
                YA[rows, :] += dh1_part(g, rows)

        return tile

    def qkv_grads(g):
        ref, w = (DA if g == 3 else G[f"q{g}"]), ZW[f"q{g}"]

        def grads(i):
            rows = tile_rows(i, 256)
            ref[rows, 0 : 3 * w] = dot(H1T[rows, :], QS[g][...]).astype(BF)

        loop(D // 256, grads)

        def sums(i):
            rows = tile_rows(i, R)
            cols = slice(128 * FIRST[g], 128 * FIRST[g] + w)
            VL[2:3, cols] += jnp.sum(QS[g][rows, 0:w].astype(F32), axis=0, keepdims=True)
            VL[3:4, cols] += jnp.sum(QS[g][rows, 2 * w :].astype(F32), axis=0, keepdims=True)

        loop(TOK // R, sums)

    for g in range(4):
        served(2 * PAIRS[g], backward_unit(g), BWD, g)
        if g < 3:
            loop(TOK // R, dh1_tile(g))
            serve(DHP, g)
            leave(f"q{g}")
        qkv_grads(g)
        serve(QG, g)
        serve(DONE, Q0 + g)

    def last_tile(i):
        rows = tile_rows(i, R)
        dh = YA[rows, :] + dh1_part(3, rows)
        xhat, r = norm_parts(TK[rows, :].astype(F32))
        VL[0:1, :] += jnp.sum(dh * xhat, axis=0, keepdims=True)
        VL[1:2, :] += jnp.sum(dh, axis=0, keepdims=True)
        YA[rows, :] = DH[rows, :] + norm_back(dh, xhat, r, gain1)

    served(TOK // R, last_tile, LAST)
    ig_copy.start()
    serve(DONE, LAST)
    serve(NEED, LAST)
    if comm:
        for n in NAMES:
            if n not in ("f0", "f1", "f2", "o", "q0", "q1", "q2"):
                gone(n)
            back_gone(n)
        links.sent(*[f"{r}{k}" for r in "el" for k in range(3)], *v_keys["e"], *v_keys["l"])
        links.sent(*[("v", d) for d in range(3)])
    else:
        vg_out[...] = VG[...]
        vl_out[...] = VL[...]
        last = []
        for i, n in enumerate(NAMES):
            src = DA.at[pl.ds(0, D), pl.ds(0, WIDTH[n])] if n == "q3" else G[n]
            last.append(pltpu.make_async_copy(src, dg_out.at[:, pl.ds(PLACE[n], WIDTH[n])], lsem.at[2 + i]))
        for k in last:
            k.start()
        for k in last:
            k.wait()
    bo_copy.wait()
    ig_copy.wait()


def run_mega(comm, lens, tok, cot, vis, *rest):
    vm = pl.BlockSpec(memory_space=pltpu.VMEM)
    hbm = pl.BlockSpec(memory_space=pl.ANY)
    smem = pl.BlockSpec(memory_space=pltpu.SMEM)
    S = jax.ShapeDtypeStruct
    V = pltpu.VMEM
    outs = [S((TOK, D), BF), S((TOK, D), F32)]
    out_specs = [hbm, hbm]
    if comm:
        outs += [S((96, D), F32), S((96, 256), F32), S((96, D), F32), S((96, D), F32), S((8, 1024), F32), S((8, D), F32)]
        out_specs += [vm] * 6
    else:
        outs += [S((D, COLS), BF), S((8, 1024), F32), S((8, D), F32)]
        out_specs += [hbm, vm, vm]
    wide, tall, flat = V((TOK, D), BF), V((D, TOK), BF), V((TOK, D), F32)
    scratch = [V((D, WIDTH[n]), BF) for n in NAMES]
    scratch += [wide, wide, tall, tall, tall, wide, wide] + [V((TOK, 384 * n), BF) for n in PAIRS] + [flat, flat]
    scratch += [V((TOK, 1024), BF), V((TOK, 1024), BF), V((2, HALF, HALF), BF), V((TOK, 128), F32)]
    scratch += [V((8, 1024), F32), V((8, D), F32), V((4, 16, 256), BF), pltpu.SemaphoreType.DMA((10,))]
    if comm:
        scratch += [V((4, 96, ZW[n]), BF) for n in NAMES[:5]]
        for rows in (384, 96, 96, 96):
            scratch += [V((rows, FCW), BF)] * 3
        scratch += [V((3, 96, ZCOLS), BF), V((3, 8, 1024), F32), V((6, 8, 1024), F32), V((3, 8, D), F32), V((6, 8, D), F32)]
        scratch += [pltpu.SemaphoreType.DMA((224,)), pltpu.SemaphoreType.DMA((224,))]
    return pl.pallas_call(
        functools.partial(mega, comm),
        out_shape=outs,
        in_specs=[smem, hbm, hbm, vm] + ([vm] * 12 if comm else [hbm, vm]),
        out_specs=out_specs,
        scratch_shapes=scratch,
        compiler_params=pltpu.CompilerParams(
            collective_id=0 if comm else None, has_side_effects=comm, vmem_limit_bytes=64 * 2**20
        ),
        cost_estimate=pl.CostEstimate(flops=60 * 10**9, bytes_accessed=20 * 10**6, transcendentals=10**7),
        name="block",
    )(lens, tok, cot, vis, *rest)


def finish(lens, bo_in, ig_in, gq_in, go_in, vg_in, vl_in, bo, ig, gg1, gs1, gq, gbqv, go, gbo, gg2, gs2, gb1, gb2, twice):
    m = lax.axis_index("mlp")
    start, _ = longest_start(lens)
    first = TOK - start
    low = lax.rem(first, 8)
    window = pl.ds(pl.multiple_of(first - low, 8), TOK + 8)
    for src, dst in ((bo_in, bo), (ig_in, ig)):
        x = src[...].astype(F32)
        twice[0:TOK, :] = x
        twice[TOK : 2 * TOK, :] = x

        def put(k, dst=dst):
            dst[...] = twice[window, :][k : k + TOK].astype(dst.dtype)

        for k in range(8):
            pl.when(low == k)(functools.partial(put, k))

    @pl.when(pl.program_id(0) == 0)
    def _():
        cat = lambda *p: jnp.concatenate(p, axis=1)
        x = gq_in[...]
        g0, g1, g2, g3 = x[:, 0:128], x[:, 128:384], x[:, 384:640], x[:, 640:768]
        gq[...] = by_device(
            m,
            [
                cat(g0, g1, g2[:, 0:192]),
                cat(g2[:, 192:256], g3, g0, g1),
                cat(g2, g3, g0, g1[:, 0:64]),
                cat(g1[:, 64:256], g2, g3),
            ],
        )
        y = go_in[...]
        go[...] = jnp.where(lax.rem(m, 2) == 0, y[:, 0:192], y[:, 64:256])
        v, u = vg_in[...], vl_in[...]
        row = lambda w, r: by_device(m, [w[r : r + 1, 192 * z : 192 * (z + 1)] for z in range(4)])
        for ref, w, r in ((gg1, u, 0), (gs1, u, 1), (gbo, v, 0), (gg2, v, 1), (gs2, v, 2), (gb2, v, 3)):
            ref[...] = row(w, r).reshape(192)
        gbqv[...] = by_device(m, [u[2:3, 0:384], u[2:3, 384:768], u[3:4, 0:384], u[3:4, 384:768]]).reshape(384)
        gb1[...] = cat(
            *[by_device(m, [v[4 + j : 5 + j, 256 * z : 256 * (z + 1)] for z in range(4)]) for j in range(3)]
        ).reshape(768)


def run_finish(lens, bo, ig, gq, go, vg, vl):
    S = jax.ShapeDtypeStruct
    f = lambda *s: S(s, F32)
    outs = [S((TOK, D), BF), f(TOK, D), f(192), f(192), f(96, 576), f(384), f(96, 192), f(192), f(192), f(192), f(768), f(192)]
    tile = pl.BlockSpec((TOK, 256), lambda i: (0, i))
    full = lambda x: pl.BlockSpec(x.shape, lambda i: (0,) * len(x.shape))
    return pl.pallas_call(
        finish,
        grid=(D // 256,),
        out_shape=outs,
        in_specs=[pl.BlockSpec(memory_space=pltpu.SMEM), tile, tile] + [full(x) for x in (gq, go, vg, vl)],
        out_specs=[tile, tile] + [full(x) for x in outs[2:]],
        scratch_shapes=[pltpu.VMEM((2 * TOK + 8, 256), F32)],
        compiler_params=pltpu.CompilerParams(vmem_limit_bytes=60 * 2**20),
        name="finish",
    )(lens, bo, ig, gq, go, vg, vl)


def body_by_collectives(tokens, clip_lengths, vis, vp, w_qkv, w_out, w_fc1, w_fc2, cotangent):
    def whole(x):
        x = lax.all_gather(x, "clips", axis=0, tiled=True)
        return lax.all_gather(x, "mlp", axis=1, tiled=False)

    n, z = w_qkv.shape[0], lax.axis_size("mlp")
    sub = w_fc1.shape[1] // 3
    q = whole(w_qkv).reshape(D, 3, D)
    q = [q[:, :, 128 * a : 128 * (a + b)].reshape(D, -1) for a, b in zip(FIRST, PAIRS)]
    o = whole(w_out).reshape(D, D)
    f = [whole(w).reshape(D, z, 3, sub).transpose(0, 2, 1, 3) for w in (w_fc1, w_fc2.T)]
    g = jnp.concatenate([*q, o, jnp.stack(f, axis=2).reshape(D, 3 * FCW)], axis=1)
    vpg = lax.all_gather(vp, "mlp", axis=0, tiled=False)
    bo, ig, dg, vg, vl = run_mega(False, clip_lengths, tokens, cotangent, vis, g, vpg)
    dg = lax.psum_scatter(dg.astype(F32), "clips", scatter_dimension=0, tiled=True)
    take = lambda n: dg[:, PLACE[n] : PLACE[n] + WIDTH[n]]
    dq = jnp.concatenate([take(f"q{g}").reshape(n, 3, -1) for g in range(4)], axis=2).reshape(n, z, -1)
    do = take("o").reshape(n, z, -1)
    df = dg[:, PLACE["f0"] :].reshape(n, 3, 2, z, sub).transpose(2, 0, 3, 1, 4).reshape(2, n, z, -1)
    cut = lambda x: lax.psum_scatter(x, "mlp", scatter_dimension=1, tiled=False)
    vg, vl = lax.psum((vg, vl), ("clips", "mlp"))
    m = lax.axis_index("mlp")
    part = lambda x: lax.dynamic_slice_in_dim(x, m * (x.shape[0] // z), x.shape[0] // z)
    row = lambda v, r: part(v[r, :D])
    gb1 = part(vg[4:7].reshape(3, z, sub).transpose(1, 0, 2).reshape(-1))
    start, _ = longest_start(clip_lengths)
    return (
        jnp.roll(bo, start, axis=0), jnp.roll(ig, start, axis=0), row(vl, 0), row(vl, 1), cut(dq),
        part(vl[2:4].reshape(-1)), cut(do), row(vg, 0), row(vg, 1), row(vg, 2), cut(df[0]), gb1, cut(df[1]).T, row(vg, 3),
    )


def body(tokens, clip_lengths, visible, ln1_gain, ln1_bias, w_qkv, b_qv, w_out, b_out, ln2_gain, ln2_bias, w_fc1, b_fc1, w_fc2, b_fc2, cotangent):
    vis = visible.reshape(1, TOK)
    vectors = (ln1_gain, ln1_bias, b_qv, b_out, ln2_gain, ln2_bias, b_fc2, b_fc1)
    if (lax.axis_size("clips"), lax.axis_size("mlp")) != (8, 4):
        return body_by_collectives(
            tokens, clip_lengths, vis, pack_vectors(vectors), w_qkv, w_out, w_fc1, w_fc2, cotangent
        )
    bo, ig, gq, go, g1, g2, vg, vl = run_mega(True, clip_lengths, tokens, cotangent, vis, w_qkv, w_out, w_fc1, w_fc2.T, *vectors)
    bo, ig, gg1, gs1, gq, gbqv, go, gbo, gg2, gs2, gb1, gb2 = run_finish(clip_lengths, bo, ig, gq, go, vg, vl)
    return (bo, ig, gg1, gs1, gq, gbqv, go, gbo, gg2, gs2, g1, gb1, g2.T, gb2)


def solution(mesh):
    in_specs = (
        P(("clips", "mlp"), None), P(("clips", "mlp"), None), P(("clips", "mlp")), P("mlp"), P("mlp"),
        P("clips", "mlp"), P("mlp"), P("clips", "mlp"), P("mlp"), P("mlp"), P("mlp"), P("clips", "mlp"),
        P("mlp"), P("mlp", "clips"), P("mlp"), P(("clips", "mlp"), None),
    )
    out_specs = (
        P(("clips", "mlp"), None), P(("clips", "mlp"), None), P("mlp"), P("mlp"), P("clips", "mlp"), P("mlp"),
        P("clips", "mlp"), P("mlp"), P("mlp"), P("mlp"), P("clips", "mlp"), P("mlp"), P("mlp", "clips"), P("mlp"),
    )
    return jax.shard_map(body, mesh=mesh, in_specs=in_specs, out_specs=out_specs, check_vma=False)
```

```python
import functools

import jax
import jax.numpy as jnp
from jax import lax
from jax.experimental import pallas as pl
from jax.experimental.pallas import tpu as pltpu
from jax.sharding import PartitionSpec as P

F32 = jnp.float32
BF = jnp.bfloat16
MESH = pl.DeviceIdType.MESH
HEADS = 12
HEAD_DIM = 64
NORM_EPS = 1e-06
MASKED = -1000000000.0
D = 768
TOK = 1024
HALF = 512
FCW = 2048
PAIRS = (1, 2, 2, 1)
FIRST = (0, 1, 3, 5)
HELD = ((0, 1, 2, None), (0, 1, 2, 2), (0, 0, 1, 2), (None, 0, 1, 2))
WIDTH = {f"q{g}": 384 * n for g, n in enumerate(PAIRS)}
WIDTH.update(o=D, f0=FCW, f1=FCW, f2=FCW)
NAMES = tuple(WIDTH)
COLS = sum(WIDTH.values())
PLACE = {n: sum(list(WIDTH.values())[:i]) for i, n in enumerate(NAMES)}
ZW = {f"q{g}": 128 * n for g, n in enumerate(PAIRS)}
ZW.update(o=256, f0=256, f1=256, f2=256)
SEGS = {n: 2 if n[0] == "f" else 1 for n in NAMES}
ZPLACE = {n: sum(ZW[k] * SEGS[k] for k in NAMES[:i]) for i, n in enumerate(NAMES)}
DIRECT = ("q0", "q1", "q2", "q3")
ZCOLS = sum(ZW[n] * SEGS[n] for n in NAMES)
R = 256
FORWARD = 128
BACKWARD = 256


def dot(a, b):
    return jnp.dot(a, b, preferred_element_type=F32)


def dot_nt(a, b):
    return lax.dot_general(a, b, (((1,), (1,)), ((), ())), preferred_element_type=F32)


def tile_rows(i, size):
    return pl.ds(pl.multiple_of(i * size, size), size)


def lanes_at(start, size):
    return pl.ds(pl.multiple_of(start, 128), size)


def loop(count, body, hooks=None):
    def step(i, carry):
        body(i)
        for k, f in (hooks or {}).items():
            pl.when(i == k)(f)
        return carry

    lax.fori_loop(0, count, step, 0)


def norm_parts(x):
    mean = jnp.mean(x, axis=-1, keepdims=True)
    centred = x - mean
    spread = jnp.mean(centred * centred, axis=-1, keepdims=True)
    r = lax.rsqrt(spread + NORM_EPS)
    return centred * r, r


def norm_back(dh, xhat, r, gain):
    e = dh * gain
    m1 = jnp.mean(e, axis=-1, keepdims=True)
    m2 = jnp.mean(e * xhat, axis=-1, keepdims=True)
    return r * (e - m1 - xhat * m2)


def gelu_parts(a):
    e = jnp.exp(a * a * -0.5)
    t = 1.0 / (1.0 + jnp.abs(a) * (0.3275911 * 0.7071067811865476))
    poly = t * (
        0.254829592
        + t * (-0.284496736 + t * (1.421413741 + t * (-1.453152027 + t * 1.061405429)))
    )
    half = 0.5 * poly * e
    phi = jnp.where(a < 0, half, 1.0 - half)
    return a * phi, phi + a * e * 0.3989422804014327


def longest_start(lens):
    n0, n1, n2, n3 = lens[0, 0], lens[0, 1], lens[0, 2], lens[0, 3]
    top = jnp.maximum(jnp.maximum(n0, n1), jnp.maximum(n2, n3))
    start = jnp.where(
        n0 == top, 0, jnp.where(n1 == top, n0, jnp.where(n2 == top, n0 + n1, n0 + n1 + n2))
    )
    return start, (n0, n0 + n1, n0 + n1 + n2)


def one_hot_cols(rows, cols, shift):
    r = lax.broadcasted_iota(jnp.int32, (rows, cols), 0)
    c = lax.broadcasted_iota(jnp.int32, (rows, cols), 1)
    return (r == c + shift).astype(BF)


class Links:
    def __init__(self, send, recv):
        self.send, self.recv, self.table = send, recv, {}

    def add(self, key, src, dst, device):
        self.table[key] = (len(self.table), src, dst, device)

    def copy(self, key):
        k, src, dst, device = self.table[key]
        return pltpu.make_async_remote_copy(
            src_ref=src(),
            dst_ref=dst(),
            send_sem=self.send.at[k],
            recv_sem=self.recv.at[k],
            device_id=device,
            device_id_type=MESH,
        )

    def start(self, *keys):
        for key in keys:
            self.copy(key).start()

    def got(self, *keys):
        for key in keys:
            self.copy(key).wait_recv()

    def sent(self, *keys):
        for key in keys:
            self.copy(key).wait_send()


def places():
    c = lax.axis_index("clips")
    m = lax.axis_index("mlp")
    bits = (lax.rem(c, 2), lax.rem(lax.div(c, 2), 2), lax.div(c, 4))
    others = [sum((1 - b if r >> i & 1 else b) * (1 << i) for i, b in enumerate(bits)) for r in range(8)]
    zs = [lax.rem(m + d, 4) for d in (1, 2, 3)]
    return c, m, bits[0], others, zs


def rows_of(c):
    return pl.ds(pl.multiple_of(c * 96, 16), 96)


def rooms(refs):
    out = {f"f{j}": ref for j, ref in enumerate(refs)}
    for n, j, at in (("o", 0, 0), ("q0", 0, 768), ("q1", 0, 1152), ("q2", 1, 0), ("q3", 1, 768)):
        out[n] = refs[j].at[:, pl.ds(at, WIDTH[n])]
    return out


def sibling_rooms(refs):
    out = {"f0": refs[0], "f1": refs[1], "f2": refs[0]}
    for n, j, at in (("o", 1, 0), ("q0", 1, 768), ("q1", 1, 1152), ("q2", 0, 0), ("q3", 0, 768)):
        out[n] = refs[j].at[:, pl.ds(at, WIDTH[n])]
    return out


def half_rows_of(c, half):
    return pl.ds(pl.multiple_of(c * 96 + 48 * half, 16), 48)


def by_device(m, values):
    out = values[3]
    for z in (2, 1, 0):
        out = jnp.where(m == z, values[z], out)
    return out


def pack_vectors(vectors):
    gain1, shift1, b_qv, b_o, gain2, shift2, b_2, b_1 = (v.astype(F32).reshape(1, -1) for v in vectors)
    pad = lambda v: jnp.concatenate([v, jnp.zeros((1, 64), F32)], axis=1)
    rows = [pad(v) for v in (gain1, shift1, b_qv[:, 0:192], b_qv[:, 192:384], b_o, gain2, shift2, b_2)]
    rows += [b_1[:, 256 * j : 256 * (j + 1)] for j in range(3)]
    line = lax.broadcasted_iota(jnp.int32, (16, 256), 0)
    out = jnp.zeros((16, 256), F32)
    for r, v in enumerate(rows):
        out = jnp.where(line == r, v, out)
    return out.astype(BF)


GZ, GM, GX, GY, GS, GF, RS, RD, RA, RB, RZ, RE, EARLY, LATE = range(14)
Q0, Q1, Q2, Q3, OUT, F0, F1, F2 = range(8)
START, PACK, ROLL, VEC, LN, T1, DY, NEED, PROJECT, FWD, MIX, T2, T3, FEED, FG, DONE, END, OT, OG, BWD, DHP, QG, LAST = range(23)
SCHEDULE = {
    (START,): ((GZ, Q1), (GZ, Q2), (GZ, OUT), (GZ, F0),),
    (LN, 0): ((GM, Q0),),
    (NEED, Q0): ((GM, Q1), (GX, Q0), (GY, Q0), (GS, Q0), (GM, Q2), (GX, Q1), (GY, Q1), (GF, Q0),),
    (FWD, 0, 1): ((GS, Q1), (GZ, Q3), (GM, OUT),),
    (NEED, Q1): ((GX, Q2), (GY, Q2), (GF, Q1),),
    (PROJECT, 1): ((GM, F0), (GS, Q2),),
    (FWD, 1, 1): ((GM, Q3), (GX, OUT), (GY, OUT), (GZ, F1), (GZ, F2),),
    (FWD, 1, 3): ((GF, Q2),),
    (NEED, Q3): ((GX, F0), (GY, F0), (GX, Q3), (GY, Q3), (GM, F1), (GS, Q3), (GS, OUT), (GF, Q3),),
    (PROJECT, 3): ((GS, F0),),
    (FWD, 3, 0): ((GF, OUT),),
    (MIX, 0): ((GM, F2),),
    (T2,): ((GF, F0),),
    (FEED, 0, 0): ((GX, F1), (GY, F1),),
    (DONE, F0): ((RS, F0),),
    (NEED, F1): ((GX, F2), (GY, F2), (GS, F1), (RD, F0), (GS, F2), (GF, F1),),
    (FEED, 1, 0): ((GF, F2),),
    (FEED, 1, 1): ((RA, F0), (RB, F0),),
    (DONE, F1): ((RS, F1),),
    (FEED, 2, 1): ((RD, F1),),
    (FG, 2, 0): ((RZ, F0),),
    (DONE, F2): ((RS, F2),),
    (END, 3): ((RA, F1), (RB, F1),),
    (OG, 0): ((RD, F2),),
    (DONE, OUT): ((RS, OUT),),
    (DONE, END): ((EARLY, 0),),
    (BWD, 0, 1): ((RE, F0),),
    (QG, 0): ((RD, OUT),),
    (DONE, Q0): ((RS, Q0),),
    (BWD, 1, 2): ((RZ, F1), (RD, Q0),),
    (BWD, 1, 3): ((RA, F2), (RB, F2),),
    (DONE, Q1): ((RS, Q1),),
    (BWD, 2, 0): ((RA, OUT), (RB, OUT), (EARLY, 1),),
    (BWD, 2, 2): ((RZ, Q0), (RD, Q1),),
    (BWD, 2, 3): ((RE, F1),),
    (QG, 2): ((EARLY, 2),),
    (DONE, Q2): ((RS, Q2),),
    (BWD, 3, 0): ((RZ, F2), (RE, Q0),),
    (BWD, 3, 1): ((RZ, OUT),),
    (QG, 3): ((RD, Q2),),
    (DONE, Q3): ((RS, Q3),),
    (LAST, 1): ((RZ, Q1), (RD, Q3),),
    (DONE, LAST): ((LATE, 0),),
    (NEED, LAST): ((RE, F2), (RZ, Q2), (RE, OUT), (RZ, Q3), (RE, Q1), (LATE, 1), (RE, Q2), (RE, Q3), (LATE, 2),),
}


def mega(comm, *refs):
    refs = list(refs)

    def take(n):
        out = refs[:n]
        del refs[:n]
        return out

    lens, tok_in, cot_in, vis = take(4)
    if comm:
        wq_in, wo_in, w1_in, w2_in = take(4)
        vec_in = take(8)
    else:
        g_in, vpg_in = take(2)
    bo_out, ig_out = take(2)
    if comm:
        gq_out, go_out, g1_out, g2_out, vg_out, vl_out = take(6)
    else:
        dg_out, vg_out, vl_out = take(3)
    G = dict(zip(NAMES, take(8)))
    TK, CT, H1T, H2T, DYT, HB, O = take(7)
    QS = take(4)
    YA, DH, H, DA, BIAS, LSE, VG, VL, VPG, lsem = take(10)
    if comm:
        Z = dict(zip(NAMES[:5], take(5)))
        SB = sibling_rooms(take(2))
        DB, XB, YB = (rooms(take(3)) for _ in range(3))
        ZB, VB, VR, UB, UR, ssem, rsem = take(7)

    grads_of = {"q0": (DA, 0), "q3": (DA, 384), "q1": (G["f0"], 0), "q2": (G["f0"], 768)}

    tok_copy = pltpu.make_async_copy(tok_in, H.at[:, pl.ds(0, D)], lsem.at[0])
    cot_copy = pltpu.make_async_copy(cot_in, DA.at[:, pl.ds(0, D)], lsem.at[1])
    bo_copy = pltpu.make_async_copy(HB, bo_out, lsem.at[0])
    ig_copy = pltpu.make_async_copy(YA, ig_out, lsem.at[1])
    tok_copy.start()
    cot_copy.start()

    if comm:
        c, m, core, others, zs = places()
        cs, cx, cy, cd = (others[r] for r in (1, 2, 4, 6))
        links = Links(ssem, rsem)
        to_s, to_x, to_y, to_d, to_z = (cs, m), (cx, m), (cy, m), (cd, m), [(c, z) for z in zs]
        partners = [(others[r], m) for r in range(1, 8)] + to_z
        barrier = pltpu.get_barrier_semaphore()
        for p in partners:
            pl.semaphore_signal(barrier, inc=1, device_id=p, device_id_type=MESH)

        def mine():
            return rows_of(c)

        def part(n, block, half=None):
            return lambda: G[n].at[rows_of(block) if half is None else half_rows_of(block, half)]

        def both(key, ref, device):
            links.add(key, ref, ref, device)

        def z_seg(n, s):
            if n[0] != "f":
                return lambda: Z[n].at[m]
            return lambda: G[n].at[mine(), lanes_at(s * 1024 + m * 256, 256)]

        z_keys, n_keys, far = {}, {}, {}
        for n in NAMES:
            z_keys[n] = [("z", n, s, d) for s in range(SEGS[n]) for d in range(3)]
            for _, _, s, d in z_keys[n]:
                both(("z", n, s, d), z_seg(n, s), to_z[d])
            both(("x", n), part(n, c), to_x)
            both(("y", n), part(n, c), to_y)
            if n in DIRECT:
                both(("dd", n), part(n, c), to_d)
            else:
                both(("dy", n), part(n, cx, 0), to_y)
                both(("dx", n), part(n, cy, 1), to_x)
            for i, block in enumerate((c, cx, cy, cd)):
                both((f"s{i}", n), part(n, block), to_s)
            far[n] = [("dd", n)] if n in DIRECT else [("dy", n), ("dx", n)]
            n_keys[n] = [(k, n) for k in ("x", "y", "s0", "s1", "s2", "s3")] + far[n]
        for d in range(3):
            both(("v", d), lambda: VPG.at[m], to_z[d])

        def gz(n):
            links.start(*z_keys[n])

        def gm(n):
            links.got(*z_keys[n])
            if n[0] == "q":
                w = ZW[n]
                for t in range(3):
                    G[n][mine(), t * w : (t + 1) * w] = sum(Z[n][z] for z in range(4) if HELD[int(n[1])][z] == t)
            elif n == "o":
                for h in range(2):
                    b, lo, hi = 384 * h, Z[n][2 * h], Z[n][2 * h + 1]
                    G[n][mine(), b : b + 128] = lo[:, 0:128]
                    G[n][mine(), b + 128 : b + 256] = lo[:, 128:256] + hi[:, 0:128]
                    G[n][mine(), b + 256 : b + 384] = hi[:, 128:256]
            links.start(("x", n), ("y", n))
            if n in DIRECT:
                links.start(*far[n])
            links.start(("s0", n))

        def gdx(n):
            links.got(("x", n))
            if n not in DIRECT:
                links.start(("dy", n))
            links.start(("s1", n))

        def gdy(n):
            links.got(("y", n))
            if n not in DIRECT:
                links.start(("dx", n))
            links.start(("s2", n))

        def gs(n):
            links.got(*far[n])
            links.start(("s3", n))

        def gf(n):
            links.got(*[(f"s{i}", n) for i in range(4)])

        def gone(n):
            links.sent(*z_keys[n], *n_keys[n])

        back = {n: (ref, 0) for n, ref in G.items()}
        back.update(grads_of)

        def z_starts(n, z):
            if n == "o":
                return [128 * (z + lax.div(z, 2))]
            if n[0] == "q":
                return [ZW[n] * by_device(z, [t or 0 for t in HELD[int(n[1])]])]
            return [256 * z, 1024 + 256 * z]

        def mem(n, block, half=None):
            rows = lambda: rows_of(block) if half is None else half_rows_of(block, half)
            return lambda: back[n][0].at[rows(), pl.ds(back[n][1], WIDTH[n])]

        def room(ref, n, half=None):
            if half is None:
                return lambda: ref[n]
            return lambda: ref[n].at[pl.ds(48 * half, 48)]

        def z_from(n, s, d):
            return lambda: back[n][0].at[mine(), lanes_at(back[n][1] + z_starts(n, zs[d])[s], ZW[n])]

        def z_room(n, s, d):
            return lambda: ZB.at[d, :, pl.ds(ZPLACE[n] + ZW[n] * s, ZW[n])]

        r_keys, far_back = {}, {}
        for n in NAMES:
            for i in range(4):
                links.add(("S", n, i), mem(n, 2 * i + 1 - core), lambda n=n, i=i: SB[n].at[pl.ds(96 * i, 96)], to_s)
            if n in DIRECT:
                links.add(("DD", n), mem(n, cd), room(DB, n), to_d)
            else:
                links.add(("DX", n), mem(n, cd, 0), room(DB, n, 0), to_x)
                links.add(("DY", n), mem(n, cd, 1), room(DB, n, 1), to_y)
            far_back[n] = [("DD", n)] if n in DIRECT else [("DX", n), ("DY", n)]
            links.add(("X", n), mem(n, cx), room(XB, n), to_x)
            links.add(("Y", n), mem(n, cy), room(YB, n), to_y)
            r_keys[n] = [("Z", n, s, d) for s in range(SEGS[n]) for d in range(3)]
            for _, _, s, d in r_keys[n]:
                links.add(("Z", n, s, d), z_from(n, s, d), z_room(n, s, d), to_z[d])

        def rS(n):
            links.start(*[("S", n, i) for i in range(4)])

        def rD(n):
            links.got(*[("S", n, i) for i in range(4)])

            def add(block):
                ref = mem(n, block)()
                other = SB[n][rows_of(lax.div(block, 2)), :]
                ref[...] = (ref[...].astype(F32) + other.astype(F32)).astype(BF)

            if n in DIRECT:
                for block in (cx, cy, cd, c):
                    add(block)
                links.start(("X", n), ("Y", n), *far_back[n])
            else:
                add(cd)
                links.start(*far_back[n])
                for block in (cx, cy, c):
                    add(block)

        def rXa(n):
            links.got(("DX", n))
            t, u = mem(n, cy, 0)(), room(DB, n, 0)()
            t[...] = (t[...].astype(F32) + u[...].astype(F32)).astype(BF)
            links.start(("Y", n))

        def rXb(n):
            links.got(("DY", n))
            t, u = mem(n, cx, 1)(), room(DB, n, 1)()
            t[...] = (t[...].astype(F32) + u[...].astype(F32)).astype(BF)
            links.start(("X", n))

        def rZ(n):
            links.got(("X", n), ("Y", n))
            rooms_in = [XB, YB]
            if n in DIRECT:
                links.got(*far_back[n])
                rooms_in.append(DB)
            t = mem(n, c)()
            t[...] = sum((room(ref, n)()[...].astype(F32) for ref in rooms_in), t[...].astype(F32)).astype(BF)
            links.start(*r_keys[n])

        def rE(n):
            links.got(*r_keys[n])
            k = 128 * FIRST[int(n[1])] if n[0] == "q" else 256 * int(n[1]) if n[0] == "f" else 0
            outs = {"o": [go_out], "q": [gq_out], "f": [g1_out, g2_out]}[n[0]]
            w = ZW[n]
            for s, out in enumerate(outs):
                total = back[n][0][mine(), lanes_at(back[n][1] + z_starts(n, m)[s], w)].astype(F32)
                for d in range(3):
                    total = total + ZB[d, :, ZPLACE[n] + w * s : ZPLACE[n] + w * (s + 1)].astype(F32)
                out[:, k : k + w] = total

        def back_gone(n):
            links.sent(*[("S", n, i) for i in range(4)], *far_back[n], ("X", n), ("Y", n), *r_keys[n])

        v_keys = {}
        for r, (src, buf, rec) in {"e": (VG, VB, VR), "l": (VL, UB, UR)}.items():
            for k in range(1, 8):
                links.add((r, k), lambda src=src: src, lambda rec=rec, k=k: rec.at[k - 1], (others[k], m))
            for d in range(3):
                links.add((r, 8 + d), lambda buf=buf: buf, lambda rec=rec, d=d: rec.at[7 + d], to_z[d])
            v_keys[r] = [[(r, k) for k in range(1, 8)], [(r, 8 + d) for d in range(3)]]

        def rv(r, k):
            src, buf, rec, out = (VG, VB, VR, vg_out) if r == "e" else (VL, UB, UR, vl_out)
            if k > 0:
                links.got(*v_keys[r][k - 1])
            if k == 1:
                buf[...] = sum((rec[i] for i in range(7)), src[...])
            if k < 2:
                links.start(*v_keys[r][k])
            else:
                out[...] = buf[...] + rec[7] + rec[8] + rec[9]

        wq = wq_in[...]
        def shard(g):
            n = f"q{g}"
            off = [
                768 * HELD[g][z] + 128 * FIRST[g] - 576 * z if HELD[g][z] is not None else -4096
                for z in range(4)
            ]
            Z[n][m] = dot(wq, one_hot_cols(576, ZW[n], by_device(m, off))).astype(BF)

        shard(0)
        VPG[m] = pack_vectors([v[...] for v in vec_in])
        pl.semaphore_wait(barrier, len(partners))
        gz("q0")
        links.start(*[("v", d) for d in range(3)])
        for g in (1, 2, 3):
            shard(g)
        Z["o"][m] = dot(wo_in[...], one_hot_cols(192, 256, jnp.where(lax.rem(m, 2) == 0, 0, -64))).astype(BF)
        for j in range(3):
            for s, w in enumerate((w1_in, w2_in)):
                G[f"f{j}"][mine(), lanes_at(s * 1024 + m * 256, 256)] = w[:, j * 256 : (j + 1) * 256]
    else:
        g_copies = [
            pltpu.make_async_copy(g_in.at[:, pl.ds(PLACE[n], WIDTH[n])], G[n], lsem.at[2 + i])
            for i, n in enumerate(NAMES)
        ]
        for k in g_copies:
            k.start()
        VPG[...] = vpg_in[...]

    def serve(*label):
        if not comm:
            return
        table = (gz, gm, gdx, gdy, gs, gf, rS, rD, rXa, rXb, rZ, rE)
        for f, n in SCHEDULE.get(label, ()):
            if f in (EARLY, LATE):
                rv("el"[f - EARLY], n)
            else:
                table[f](NAMES[n])

    def leave(n):
        if comm:
            gone(n)

    def served(count, body, *label):
        hooks = {i: functools.partial(serve, *label, i) for i in range(count) if (*label, i) in SCHEDULE}
        loop(count, body, hooks if comm else None)

    start, ends = longest_start(lens)
    tok_copy.wait()
    cot_copy.wait()
    vis8 = jnp.broadcast_to(vis[...], (8, TOK)).astype(F32).astype(BF)

    def roll_tile(i):
        rows = tile_rows(i, R)
        place = lax.broadcasted_iota(jnp.int32, (R, 1), 0) + i * R + start
        place = jnp.where(place >= TOK, place - TOK, place)
        perm = (lax.broadcasted_iota(jnp.int32, (R, TOK), 1) == place).astype(BF)
        TK[rows, :] = dot(perm, H[:, 0:D]).astype(BF)
        CT[rows, :] = dot(perm, DA[:, 0:D]).astype(BF)
        clip = sum((place >= e).astype(jnp.int32) for e in ends)
        spot = lax.broadcasted_iota(jnp.int32, (R, 1), 0) + lax.rem(i, 2) * R
        key = lax.broadcasted_iota(jnp.int32, (1, HALF), 1)
        far = key + lax.div(i, 2) * HALF + start
        far = jnp.where(far >= TOK, far - TOK, far)
        clip_k = sum((far >= e).astype(jnp.int32) for e in ends)
        whole = lax.broadcasted_iota(jnp.int32, (HALF, TOK), 0) + lax.div(i, 2) * HALF + start
        whole = jnp.where(whole >= TOK, whole - TOK, whole)
        keys = (lax.broadcasted_iota(jnp.int32, (HALF, TOK), 1) == whole).astype(BF)
        seen = dot_nt(vis8, keys)[0:1, :]
        allowed = (clip == clip_k) & ((seen > 0.5) | (key == spot))
        BIAS[lax.div(i, 2), tile_rows(lax.rem(i, 2), R), :] = jnp.where(
            allowed, 0.0, MASKED
        ).astype(BF)

    serve(START)
    serve(PACK)
    served(TOK // R, roll_tile, ROLL)

    if comm:
        links.got(*[("v", d) for d in range(3)])

    def spread(parts):
        return sum(dot(VPG[z][r : r + 1, :], place_of[p]) for z, r, p in parts)

    place_of = [
        (
            (
                lax.broadcasted_iota(jnp.int32, (256, D), 0) + 192 * p
                == lax.broadcasted_iota(jnp.int32, (256, D), 1)
            )
            & (lax.broadcasted_iota(jnp.int32, (256, D), 0) < 192)
        ).astype(BF)
        for p in range(4)
    ]
    each = lambda r: [(z, r, z) for z in range(4)]
    gain1, shift1 = spread(each(0)), spread(each(1))
    bias_q = spread([(0, 2, 0), (0, 3, 1), (1, 2, 2), (1, 3, 3)])
    bias_v = spread([(2, 2, 0), (2, 3, 1), (3, 2, 2), (3, 3, 3)])
    bias_o, gain2, shift2, bias_2 = (spread(each(r)) for r in (4, 5, 6, 7))
    bias_1 = [
        jnp.concatenate([VPG[z][8 + j : 9 + j, :].astype(F32) for z in range(4)], axis=1)
        for j in range(3)
    ]

    serve(VEC)

    def ln1_tile(i):
        rows = tile_rows(i, R)
        xhat, _ = norm_parts(TK[rows, :].astype(F32))
        HB[rows, :] = (xhat * gain1 + shift1).astype(BF)

    served(TOK // R, ln1_tile, LN)
    H1T[...] = HB[...].T
    LSE[...] = jnp.zeros_like(LSE)
    serve(T1)
    VG[...] = jnp.zeros_like(VG)
    VL[...] = jnp.zeros_like(VL)

    def dy_tile(i):
        VG[3:4, 0:D] += jnp.sum(CT[tile_rows(i, R), :].astype(F32), axis=0, keepdims=True)

    loop(TOK // R, dy_tile)
    serve(DY)
    if not comm:
        for k in g_copies:
            k.wait()

    def project(g):
        def tile(i):
            rows = tile_rows(i, 512)
            p = dot(HB[rows, :], G[f"q{g}"][...])
            w = ZW[f"q{g}"]
            cols = slice(128 * FIRST[g], 128 * FIRST[g] + w)
            QS[g][rows, 0:w] = ((p[:, 0:w] + bias_q[:, cols]).astype(BF) * 0.125).astype(BF)
            QS[g][rows, w : 2 * w] = p[:, w : 2 * w].astype(BF)
            QS[g][rows, 2 * w :] = (p[:, 2 * w :] + bias_v[:, cols]).astype(BF)

        loop(TOK // 512, tile)

    lane = lax.broadcasted_iota(jnp.int32, (1, 128), 1)
    sides = [lane < 64, lane >= 64]

    def unit_of(u):
        return lax.div(u, 2), lax.rem(u, 2)

    def two_heads(x):
        return jnp.concatenate([jnp.where(sides[0], x, 0), jnp.where(sides[1], x, 0)], axis=0).astype(BF)

    def twice(x):
        return jnp.concatenate([x, x], axis=0)

    def forward_unit(g):
        def unit(u):
            p, half = unit_of(u)
            rows = tile_rows(half, HALF)
            head = 2 * (FIRST[g] + p)
            k = QS[g][rows, lanes_at(ZW[f"q{g}"] + p * 128, 128)]
            v = QS[g][rows, lanes_at(2 * ZW[f"q{g}"] + p * 128, 128)]
            v1 = jnp.concatenate([v, jnp.ones((HALF, 128), BF)], axis=1)
            for a in range(0, HALF, FORWARD):
                some = pl.ds(pl.multiple_of(half * HALF + a, FORWARD), FORWARD)
                q = QS[g][some, lanes_at(p * 128, 128)]
                s = dot_nt(two_heads(q), k) + twice(BIAS[half, a : a + FORWARD, :].astype(F32))
                top = jnp.max(s, axis=1, keepdims=True)
                out = dot(jnp.exp(s - top).astype(BF), v1)
                even, odd = out[:FORWARD], out[FORWARD:]
                total = jnp.where(sides[0], even[:, 128:], odd[:, 128:])
                O[some, lanes_at((FIRST[g] + p) * 128, 128)] = (
                    jnp.where(sides[0], even[:, :128], odd[:, :128]) / total
                ).astype(BF)
                LSE[some, :] = jnp.where(
                    lane == head,
                    top[:FORWARD] + jnp.log(even[:, 128:]),
                    jnp.where(lane == head + 1, top[FORWARD:] + jnp.log(odd[:, 128:]), LSE[some, :]),
                )

        return unit

    def backward_unit(g):
        def unit(u):
            p, half = unit_of(u)
            rows = tile_rows(half, HALF)
            at_q, at_k, at_v = (lanes_at(b * ZW[f"q{g}"] + p * 128, 128) for b in range(3))
            at_o = lanes_at((FIRST[g] + p) * 128, 128)
            head = 2 * (FIRST[g] + p)
            k, v = QS[g][rows, at_k], QS[g][rows, at_v]
            dk = dv = 0.0
            for a in range(0, HALF, BACKWARD):
                some = pl.ds(pl.multiple_of(half * HALF + a, BACKWARD), BACKWARD)
                q, do = two_heads(QS[g][some, at_q]), two_heads(H[some, at_o])
                both = H[some, at_o].astype(F32) * O[some, at_o].astype(F32)
                pick = lambda which, x: jnp.sum(jnp.where(which, x, 0.0), axis=1, keepdims=True)
                delta = jnp.concatenate([pick(sides[0], both), pick(sides[1], both)], axis=0)
                lse = LSE[some, :]
                lse = jnp.concatenate([pick(lane == head, lse), pick(lane == head + 1, lse)], axis=0)
                s = dot_nt(q, k) + twice(BIAS[half, a : a + BACKWARD, :].astype(F32))
                w = jnp.exp(s - lse)
                ds = (w * (dot_nt(do, v) - delta)).astype(BF)
                w = w.astype(BF)
                dq = dot(ds, k)
                QS[g][some, at_q] = (jnp.where(sides[0], dq[:BACKWARD], dq[BACKWARD:]) * 0.125).astype(BF)
                dk = dk + dot(q.T, ds)
                dv = dv + dot(do.T, w)
            QS[g][rows, at_k] = dk.astype(BF).T
            QS[g][rows, at_v] = dv.astype(BF).T

        return unit

    for g in range(4):
        serve(NEED, Q0 + g)
        project(g)
        serve(PROJECT, g)
        served(2 * PAIRS[g], forward_unit(g), FWD, g)
    serve(NEED, OUT)

    def mixed(rows):
        return TK[rows, :].astype(F32) + dot(O[rows, :], G["o"][...]) + bias_o

    def mix_tile(i):
        rows = tile_rows(i, R)
        x2 = mixed(rows)
        xhat, _ = norm_parts(x2)
        HB[rows, :] = (xhat * gain2 + shift2).astype(BF)

    served(TOK // R, mix_tile, MIX)
    H2T[...] = HB[...].T
    serve(T2)
    DYT[...] = CT[...].T
    serve(T3)

    def feed(j):
        W1 = lambda: G[f"f{j}"][:, 0:1024]
        W2 = lambda: G[f"f{j}"][:, 1024:]
        for rows in (slice(0, 512), slice(512, TOK)):
            act, slope = gelu_parts(dot(HB[rows, :], W1()) + bias_1[j])
            H[rows, :] = act.astype(BF)
            da = (dot(CT[rows, :], W2()) * slope).astype(BF)
            DA[rows, :] = da
            VG[4 + j : 5 + j, :] += jnp.sum(da.astype(F32), axis=0, keepdims=True)
        serve(FEED, j, 0)
        if j == 0:
            YA[...] = dot_nt(H[...], W2())
            DH[...] = dot_nt(DA[...], W1())
        else:
            YA[...] += dot_nt(H[...], W2())
            DH[...] += dot_nt(DA[...], W1())
        serve(FEED, j, 1)

    def feed_grads(j):
        G[f"f{j}"][:, 0:1024] = dot(H2T[...], DA[...]).astype(BF)
        G[f"f{j}"][:, 1024:] = dot(DYT[...], H[...]).astype(BF)

    for j in range(3):
        serve(NEED, F0 + j)
        feed(j)
        leave(f"f{j}")
        feed_grads(j)
        serve(FG, j, 0)
        serve(DONE, F0 + j)

    def end_tile(i):
        rows = tile_rows(i, R)
        x2 = mixed(rows)
        HB[rows, :] = (x2 + YA[rows, :] + bias_2).astype(BF)
        xhat, r = norm_parts(x2)
        dh = DH[rows, :]
        VG[1:2, 0:D] += jnp.sum(dh * xhat, axis=0, keepdims=True)
        VG[2:3, 0:D] += jnp.sum(dh, axis=0, keepdims=True)
        dx2 = CT[rows, :].astype(F32) + norm_back(dh, xhat, r, gain2)
        DH[rows, :] = dx2
        dz = dx2.astype(BF)
        CT[rows, :] = dz
        VG[0:1, 0:D] += jnp.sum(dz.astype(F32), axis=0, keepdims=True)
        H[rows, 0:D] = dot_nt(dz, G["o"][...]).astype(BF)

    served(TOK // R, end_tile, END)
    bo_copy.start()
    if not comm:
        f0_copy = pltpu.make_async_copy(G["f0"], dg_out.at[:, pl.ds(PLACE["f0"], FCW)], lsem.at[2])
        f0_copy.start()
    H2T[...] = O[...].T
    serve(OT)
    leave("o")

    G["o"][...] = dot(H2T[...], CT[...]).astype(BF)
    serve(OG, 0)
    serve(DONE, OUT)
    serve(DONE, END)

    def qkv_grads(g):
        (ref, at), w = grads_of[f"q{g}"], ZW[f"q{g}"]
        ref[0:D, at : at + 3 * w] = dot(H1T[...], QS[g][...]).astype(BF)
        cols = slice(128 * FIRST[g], 128 * FIRST[g] + w)

        def sums(i):
            rows = tile_rows(i, R)
            VL[2:3, cols] += jnp.sum(QS[g][rows, 0:w].astype(F32), axis=0, keepdims=True)
            VL[3:4, cols] += jnp.sum(QS[g][rows, 2 * w :].astype(F32), axis=0, keepdims=True)

        loop(TOK // R, sums)

    for g in range(4):
        served(2 * PAIRS[g], backward_unit(g), BWD, g)
        if g == 1 and comm:
            serve(NEED, RE)
            back_gone("f0")
        if g == 1 and not comm:
            f0_copy.wait()
        qkv_grads(g)
        serve(QG, g)
        serve(DONE, Q0 + g)

    def last_tile(i):
        rows = tile_rows(i, 512)
        dh = sum(dot_nt(QS[g][rows, :], G[f"q{g}"][...]) for g in range(4))
        xhat, r = norm_parts(TK[rows, :].astype(F32))
        VL[0:1, :] += jnp.sum(dh * xhat, axis=0, keepdims=True)
        VL[1:2, :] += jnp.sum(dh, axis=0, keepdims=True)
        YA[rows, :] = DH[rows, :] + norm_back(dh, xhat, r, gain1)

    served(TOK // 512, last_tile, LAST)
    ig_copy.start()
    serve(DONE, LAST)
    serve(NEED, LAST)
    if comm:
        for n in NAMES:
            if n[0] == "q":
                gone(n)
            if n != "f0":
                back_gone(n)
        for r in "el":
            links.sent(*v_keys[r][0], *v_keys[r][1])
        links.sent(*[("v", d) for d in range(3)])
    else:
        vg_out[...] = VG[...]
        vl_out[...] = VL[...]
        last = []
        for i, n in enumerate(NAMES):
            if n == "f0":
                continue
            ref, at = grads_of.get(n, (G[n], 0))
            src = ref.at[pl.ds(0, D), pl.ds(at, WIDTH[n])]
            last.append(pltpu.make_async_copy(src, dg_out.at[:, pl.ds(PLACE[n], WIDTH[n])], lsem.at[2 + i]))
        for k in last:
            k.start()
        for k in last:
            k.wait()
    bo_copy.wait()
    ig_copy.wait()


def run_mega(comm, lens, tok, cot, vis, *rest):
    vm = pl.BlockSpec(memory_space=pltpu.VMEM)
    hbm = pl.BlockSpec(memory_space=pl.ANY)
    smem = pl.BlockSpec(memory_space=pltpu.SMEM)
    S = jax.ShapeDtypeStruct
    V = pltpu.VMEM
    outs = [S((TOK, D), BF), S((TOK, D), F32)]
    out_specs = [hbm, hbm]
    if comm:
        outs += [S((96, D), F32), S((96, 256), F32), S((96, D), F32), S((96, D), F32), S((8, 1024), F32), S((8, D), F32)]
        out_specs += [vm] * 6
    else:
        outs += [S((D, COLS), BF), S((8, 1024), F32), S((8, D), F32)]
        out_specs += [hbm, vm, vm]
    wide, tall, flat = V((TOK, D), BF), V((D, TOK), BF), V((TOK, D), F32)
    scratch = [V((D, WIDTH[n]), BF) for n in NAMES]
    scratch += [wide, wide, tall, tall, tall, wide, wide] + [V((TOK, 384 * n), BF) for n in PAIRS] + [flat, flat]
    scratch += [V((TOK, 1024), BF), V((TOK, 1024), BF), V((2, HALF, HALF), BF), V((TOK, 128), F32)]
    scratch += [V((8, 1024), F32), V((8, D), F32), V((4, 16, 256), BF), pltpu.SemaphoreType.DMA((10,))]
    if comm:
        scratch += [V((4, 96, ZW[n]), BF) for n in NAMES[:5]]
        scratch += [V((384, FCW), BF)] * 2 + [V((96, FCW), BF)] * 9
        scratch += [V((3, 96, ZCOLS), BF), V((8, 1024), F32), V((10, 8, 1024), F32), V((8, D), F32), V((10, 8, D), F32)]
        scratch += [pltpu.SemaphoreType.DMA((224,)), pltpu.SemaphoreType.DMA((224,))]
    return pl.pallas_call(
        functools.partial(mega, comm),
        out_shape=outs,
        in_specs=[smem, hbm, hbm, vm] + ([vm] * 12 if comm else [hbm, vm]),
        out_specs=out_specs,
        scratch_shapes=scratch,
        compiler_params=pltpu.CompilerParams(
            collective_id=0 if comm else None, has_side_effects=comm, vmem_limit_bytes=64 * 2**20
        ),
        cost_estimate=pl.CostEstimate(flops=60 * 10**9, bytes_accessed=20 * 10**6, transcendentals=10**7),
        name="block",
    )(lens, tok, cot, vis, *rest)


def finish(lens, bo_in, ig_in, gq_in, go_in, g1_in, g2_in, vg_in, vl_in, bo, ig, gg1, gs1, gq, gbqv, go, gbo, gg2, gs2, g1, gb1, g2, gb2, twice):
    m = lax.axis_index("mlp")
    start, _ = longest_start(lens)
    first = TOK - start
    low = lax.rem(first, 8)
    window = pl.ds(pl.multiple_of(first - low, 8), TOK + 8)
    for src, dst in ((bo_in, bo), (ig_in, ig)):
        x = src[...].astype(F32)
        twice[0:TOK, :] = x
        twice[TOK : 2 * TOK, :] = x

        def put(k, dst=dst):
            dst[...] = twice[window, :][k : k + TOK].astype(dst.dtype)

        for k in range(8):
            pl.when(low == k)(functools.partial(put, k))

    @pl.when(pl.program_id(0) == 0)
    def _():
        cat = lambda *p: jnp.concatenate(p, axis=1)
        x = gq_in[...]
        p0, p1, p2, p3 = x[:, 0:128], x[:, 128:384], x[:, 384:640], x[:, 640:768]
        gq[...] = by_device(
            m,
            [
                cat(p0, p1, p2[:, 0:192]),
                cat(p2[:, 192:256], p3, p0, p1),
                cat(p2, p3, p0, p1[:, 0:64]),
                cat(p1[:, 64:256], p2, p3),
            ],
        )
        g1[...] = g1_in[...]
        g2[...] = g2_in[...]
        y = go_in[...]
        go[...] = jnp.where(lax.rem(m, 2) == 0, y[:, 0:192], y[:, 64:256])
        v, u = vg_in[...], vl_in[...]
        row = lambda w, r: by_device(m, [w[r : r + 1, 192 * z : 192 * (z + 1)] for z in range(4)])
        for ref, w, r in ((gg1, u, 0), (gs1, u, 1), (gbo, v, 0), (gg2, v, 1), (gs2, v, 2), (gb2, v, 3)):
            ref[...] = row(w, r).reshape(192)
        gbqv[...] = by_device(m, [u[2:3, 0:384], u[2:3, 384:768], u[3:4, 0:384], u[3:4, 384:768]]).reshape(384)
        gb1[...] = cat(
            *[by_device(m, [v[4 + j : 5 + j, 256 * z : 256 * (z + 1)] for z in range(4)]) for j in range(3)]
        ).reshape(768)


def run_finish(lens, bo, ig, gq, go, g1, g2, vg, vl):
    S = jax.ShapeDtypeStruct
    f = lambda *s: S(s, F32)
    outs = [S((TOK, D), BF), f(TOK, D), f(192), f(192), f(96, 576), f(384), f(96, 192), f(192), f(192), f(192), f(96, D), f(768), f(96, D), f(192)]
    tile = pl.BlockSpec((TOK, 384), lambda i: (0, i))
    full = lambda x: pl.BlockSpec(x.shape, lambda i: (0,) * len(x.shape))
    return pl.pallas_call(
        finish,
        grid=(D // 384,),
        out_shape=outs,
        in_specs=[pl.BlockSpec(memory_space=pltpu.SMEM), tile, tile] + [full(x) for x in (gq, go, g1, g2, vg, vl)],
        out_specs=[tile, tile] + [full(x) for x in outs[2:]],
        scratch_shapes=[pltpu.VMEM((2 * TOK + 8, 384), F32)],
        compiler_params=pltpu.CompilerParams(vmem_limit_bytes=60 * 2**20),
        name="finish",
    )(lens, bo, ig, gq, go, g1, g2, vg, vl)


def body_by_collectives(tokens, clip_lengths, vis, vp, w_qkv, w_out, w_fc1, w_fc2, cotangent):
    def whole(x):
        x = lax.all_gather(x, "clips", axis=0, tiled=True)
        return lax.all_gather(x, "mlp", axis=1, tiled=False)

    n, z = w_qkv.shape[0], lax.axis_size("mlp")
    sub = w_fc1.shape[1] // 3
    q = whole(w_qkv).reshape(D, 3, D)
    q = [q[:, :, 128 * a : 128 * (a + b)].reshape(D, -1) for a, b in zip(FIRST, PAIRS)]
    o = whole(w_out).reshape(D, D)
    f = [whole(w).reshape(D, z, 3, sub).transpose(0, 2, 1, 3) for w in (w_fc1, w_fc2.T)]
    g = jnp.concatenate([*q, o, jnp.stack(f, axis=2).reshape(D, 3 * FCW)], axis=1)
    vpg = lax.all_gather(vp, "mlp", axis=0, tiled=False)
    bo, ig, dg, vg, vl = run_mega(False, clip_lengths, tokens, cotangent, vis, g, vpg)
    dg = lax.psum_scatter(dg.astype(F32), "clips", scatter_dimension=0, tiled=True)
    take = lambda n: dg[:, PLACE[n] : PLACE[n] + WIDTH[n]]
    dq = jnp.concatenate([take(f"q{g}").reshape(n, 3, -1) for g in range(4)], axis=2).reshape(n, z, -1)
    do = take("o").reshape(n, z, -1)
    df = dg[:, PLACE["f0"] :].reshape(n, 3, 2, z, sub).transpose(2, 0, 3, 1, 4).reshape(2, n, z, -1)
    cut = lambda x: lax.psum_scatter(x, "mlp", scatter_dimension=1, tiled=False)
    vg, vl = lax.psum((vg, vl), ("clips", "mlp"))
    m = lax.axis_index("mlp")
    part = lambda x: lax.dynamic_slice_in_dim(x, m * (x.shape[0] // z), x.shape[0] // z)
    row = lambda v, r: part(v[r, :D])
    gb1 = part(vg[4:7].reshape(3, z, sub).transpose(1, 0, 2).reshape(-1))
    start, _ = longest_start(clip_lengths)
    return (
        jnp.roll(bo, start, axis=0), jnp.roll(ig, start, axis=0), row(vl, 0), row(vl, 1), cut(dq),
        part(vl[2:4].reshape(-1)), cut(do), row(vg, 0), row(vg, 1), row(vg, 2), cut(df[0]), gb1, cut(df[1]).T, row(vg, 3),
    )


def body(tokens, clip_lengths, visible, ln1_gain, ln1_bias, w_qkv, b_qv, w_out, b_out, ln2_gain, ln2_bias, w_fc1, b_fc1, w_fc2, b_fc2, cotangent):
    vis = visible.reshape(1, TOK)
    vectors = (ln1_gain, ln1_bias, b_qv, b_out, ln2_gain, ln2_bias, b_fc2, b_fc1)
    if (lax.axis_size("clips"), lax.axis_size("mlp")) != (8, 4):
        return body_by_collectives(
            tokens, clip_lengths, vis, pack_vectors(vectors), w_qkv, w_out, w_fc1, w_fc2, cotangent
        )
    bo, ig, gq, go, g1, g2, vg, vl = run_mega(True, clip_lengths, tokens, cotangent, vis, w_qkv, w_out, w_fc1, w_fc2.T, *vectors)
    bo, ig, gg1, gs1, gq, gbqv, go, gbo, gg2, gs2, g1, gb1, g2, gb2 = run_finish(
        clip_lengths, bo, ig, gq, go, g1, g2, vg, vl
    )
    return (bo, ig, gg1, gs1, gq, gbqv, go, gbo, gg2, gs2, g1, gb1, g2.T, gb2)


def solution(mesh):
    in_specs = (
        P(("clips", "mlp"), None), P(("clips", "mlp"), None), P(("clips", "mlp")), P("mlp"), P("mlp"),
        P("clips", "mlp"), P("mlp"), P("clips", "mlp"), P("mlp"), P("mlp"), P("mlp"), P("clips", "mlp"),
        P("mlp"), P("mlp", "clips"), P("mlp"), P(("clips", "mlp"), None),
    )
    out_specs = (
        P(("clips", "mlp"), None), P(("clips", "mlp"), None), P("mlp"), P("mlp"), P("clips", "mlp"), P("mlp"),
        P("clips", "mlp"), P("mlp"), P("mlp"), P("mlp"), P("clips", "mlp"), P("mlp"), P("mlp", "clips"), P("mlp"),
    )
    return jax.shard_map(body, mesh=mesh, in_specs=in_specs, out_specs=out_specs, check_vma=False)
```

```python
import functools

import jax
import jax.numpy as jnp
from jax import lax
from jax.experimental import pallas as pl
from jax.experimental.pallas import tpu as pltpu
from jax.sharding import PartitionSpec as P

F32 = jnp.float32
BF = jnp.bfloat16
MESH = pl.DeviceIdType.MESH
HEADS = 12
HEAD_DIM = 64
NORM_EPS = 1e-06
MASKED = -1000000000.0
D = 768
TOK = 1024
HALF = 512
FCW = 2048
PAIRS = (1, 2, 2, 1)
FIRST = (0, 1, 3, 5)
HELD = ((0, 1, 2, None), (0, 1, 2, 2), (0, 0, 1, 2), (None, 0, 1, 2))
WIDTH = {f"q{g}": 384 * n for g, n in enumerate(PAIRS)}
WIDTH.update(o=D, f0=FCW, f1=FCW, f2=FCW)
NAMES = tuple(WIDTH)
COLS = sum(WIDTH.values())
PLACE = {n: sum(list(WIDTH.values())[:i]) for i, n in enumerate(NAMES)}
ZW = {f"q{g}": 128 * n for g, n in enumerate(PAIRS)}
ZW.update(o=256, f0=256, f1=256, f2=256)
SEGS = {n: 2 if n[0] == "f" else 1 for n in NAMES}
ZPLACE = {n: sum(ZW[k] * SEGS[k] for k in NAMES[:i]) for i, n in enumerate(NAMES)}
DIRECT = ("q0", "q1", "q2", "q3")
ZCOLS = sum(ZW[n] * SEGS[n] for n in NAMES)
R = 256
FORWARD = 128
BACKWARD = 256


def dot(a, b):
    return jnp.dot(a, b, preferred_element_type=F32)


def dot_nt(a, b):
    return lax.dot_general(a, b, (((1,), (1,)), ((), ())), preferred_element_type=F32)


def tile_rows(i, size):
    return pl.ds(pl.multiple_of(i * size, size), size)


def lanes_at(start, size):
    return pl.ds(pl.multiple_of(start, 128), size)


def loop(count, body, hooks=None):
    def step(i, carry):
        body(i)
        for k, f in (hooks or {}).items():
            pl.when(i == k)(f)
        return carry

    lax.fori_loop(0, count, step, 0)


def norm_parts(x):
    mean = jnp.mean(x, axis=-1, keepdims=True)
    centred = x - mean
    spread = jnp.mean(centred * centred, axis=-1, keepdims=True)
    r = lax.rsqrt(spread + NORM_EPS)
    return centred * r, r


def norm_back(dh, xhat, r, gain):
    e = dh * gain
    m1 = jnp.mean(e, axis=-1, keepdims=True)
    m2 = jnp.mean(e * xhat, axis=-1, keepdims=True)
    return r * (e - m1 - xhat * m2)


def gelu_parts(a):
    e = jnp.exp(a * a * -0.5)
    t = 1.0 / (1.0 + jnp.abs(a) * (0.3275911 * 0.7071067811865476))
    poly = t * (
        0.254829592
        + t * (-0.284496736 + t * (1.421413741 + t * (-1.453152027 + t * 1.061405429)))
    )
    half = 0.5 * poly * e
    phi = jnp.where(a < 0, half, 1.0 - half)
    return a * phi, phi + a * e * 0.3989422804014327


def longest_start(lens):
    n0, n1, n2, n3 = lens[0, 0], lens[0, 1], lens[0, 2], lens[0, 3]
    top = jnp.maximum(jnp.maximum(n0, n1), jnp.maximum(n2, n3))
    start = jnp.where(
        n0 == top, 0, jnp.where(n1 == top, n0, jnp.where(n2 == top, n0 + n1, n0 + n1 + n2))
    )
    return start, (n0, n0 + n1, n0 + n1 + n2)


def one_hot_cols(rows, cols, shift):
    r = lax.broadcasted_iota(jnp.int32, (rows, cols), 0)
    c = lax.broadcasted_iota(jnp.int32, (rows, cols), 1)
    return (r == c + shift).astype(BF)


class Links:
    def __init__(self, send, recv):
        self.send, self.recv, self.table = send, recv, {}

    def add(self, key, src, dst, device):
        self.table[key] = (len(self.table), src, dst, device)

    def copy(self, key):
        k, src, dst, device = self.table[key]
        return pltpu.make_async_remote_copy(
            src_ref=src(),
            dst_ref=dst(),
            send_sem=self.send.at[k],
            recv_sem=self.recv.at[k],
            device_id=device,
            device_id_type=MESH,
        )

    def start(self, *keys):
        for key in keys:
            self.copy(key).start()

    def got(self, *keys):
        for key in keys:
            self.copy(key).wait_recv()

    def sent(self, *keys):
        for key in keys:
            self.copy(key).wait_send()


def places():
    c = lax.axis_index("clips")
    m = lax.axis_index("mlp")
    bits = (lax.rem(c, 2), lax.rem(lax.div(c, 2), 2), lax.div(c, 4))
    others = [sum((1 - b if r >> i & 1 else b) * (1 << i) for i, b in enumerate(bits)) for r in range(8)]
    zs = [lax.rem(m + d, 4) for d in (2, 3, 1)]
    return c, m, bits[0], others, zs


def rows_of(c):
    return pl.ds(pl.multiple_of(c * 96, 16), 96)


def rooms(refs):
    out = {f"f{j}": ref for j, ref in enumerate(refs)}
    for n, j, at in (("o", 0, 0), ("q0", 0, 768), ("q1", 0, 1152), ("q2", 1, 0), ("q3", 1, 768)):
        out[n] = refs[j].at[:, pl.ds(at, WIDTH[n])]
    return out


def sibling_rooms(refs):
    out = {"f0": refs[0], "f1": refs[1], "f2": refs[0]}
    for n, j, at in (("o", 1, 0), ("q0", 1, 768), ("q1", 1, 1152), ("q2", 0, 0), ("q3", 0, 768)):
        out[n] = refs[j].at[:, pl.ds(at, WIDTH[n])]
    return out


def half_rows_of(c, half):
    return pl.ds(pl.multiple_of(c * 96 + 48 * half, 16), 48)


def by_device(m, values):
    out = values[3]
    for z in (2, 1, 0):
        out = jnp.where(m == z, values[z], out)
    return out


def pack_vectors(vectors):
    gain1, shift1, b_qv, b_o, gain2, shift2, b_2, b_1 = (v.astype(F32).reshape(1, -1) for v in vectors)
    pad = lambda v: jnp.concatenate([v, jnp.zeros((1, 64), F32)], axis=1)
    rows = [pad(v) for v in (gain1, shift1, b_qv[:, 0:192], b_qv[:, 192:384], b_o, gain2, shift2, b_2)]
    rows += [b_1[:, 256 * j : 256 * (j + 1)] for j in range(3)]
    line = lax.broadcasted_iota(jnp.int32, (16, 256), 0)
    out = jnp.zeros((16, 256), F32)
    for r, v in enumerate(rows):
        out = jnp.where(line == r, v, out)
    return out.astype(BF)


GZ, GM, GX, GY, GS, GF, RS, RD, RA, RB, RZ, RE, EARLY, LATE = range(14)
Q0, Q1, Q2, Q3, OUT, F0, F1, F2 = range(8)
START, PACK, ROLL, VEC, LN, T1, DY, NEED, PROJECT, FWD, MIX, T2, T3, FEED, FG, DONE, END, OT, OG, BWD, DHP, QG, LAST = range(23)
SCHEDULE = {
    (START,): ((GZ, Q1), (GZ, Q2), (GZ, OUT), (GZ, F0),),
    (LN, 0): ((GM, Q0),),
    (NEED, Q0): ((GM, Q1), (GX, Q0), (GY, Q0), (GS, Q0), (GM, Q2), (GX, Q1), (GY, Q1), (GF, Q0),),
    (FWD, 0, 1): ((GS, Q1), (GZ, Q3), (GM, OUT),),
    (NEED, Q1): ((GX, Q2), (GY, Q2), (GF, Q1),),
    (PROJECT, 1): ((GM, F0), (GS, Q2),),
    (FWD, 1, 1): ((GM, Q3), (GX, OUT), (GY, OUT), (GZ, F1), (GZ, F2),),
    (FWD, 1, 3): ((GF, Q2),),
    (NEED, Q3): ((GX, F0), (GY, F0), (GX, Q3), (GY, Q3), (GM, F1), (GS, Q3), (GS, OUT), (GF, Q3),),
    (PROJECT, 3): ((GS, F0),),
    (FWD, 3, 0): ((GF, OUT),),
    (MIX, 0): ((GM, F2),),
    (T2,): ((GF, F0),),
    (FEED, 0, 0): ((GX, F1), (GY, F1),),
    (DONE, F0): ((RS, F0),),
    (NEED, F1): ((GX, F2), (GY, F2), (GS, F1), (RD, F0), (GS, F2), (GF, F1),),
    (FEED, 1, 0): ((GF, F2),),
    (FEED, 1, 1): ((RA, F0), (RB, F0),),
    (DONE, F1): ((RS, F1),),
    (FEED, 2, 1): ((RD, F1),),
    (FG, 2, 0): ((RZ, F0),),
    (DONE, F2): ((RS, F2),),
    (END, 3): ((RA, F1), (RB, F1),),
    (OG, 0): ((RD, F2),),
    (DONE, OUT): ((RS, OUT),),
    (DONE, END): ((EARLY, 0),),
    (BWD, 0, 1): ((RE, F0),),
    (QG, 0): ((RD, OUT),),
    (DONE, Q0): ((RS, Q0),),
    (BWD, 1, 2): ((RZ, F1), (RD, Q0),),
    (BWD, 1, 3): ((RA, F2), (RB, F2),),
    (DONE, Q1): ((RS, Q1),),
    (BWD, 2, 0): ((RA, OUT), (RB, OUT), (EARLY, 1),),
    (BWD, 2, 2): ((RZ, Q0), (RD, Q1),),
    (BWD, 2, 3): ((RE, F1),),
    (QG, 2): ((EARLY, 2),),
    (DONE, Q2): ((RS, Q2),),
    (BWD, 3, 0): ((RZ, F2), (RE, Q0),),
    (BWD, 3, 1): ((RZ, OUT),),
    (QG, 3): ((RD, Q2),),
    (DONE, Q3): ((RS, Q3),),
    (LAST, 1): ((RZ, Q1), (RD, Q3),),
    (DONE, LAST): ((LATE, 0),),
    (NEED, LAST): ((RE, F2), (RZ, Q2), (RE, OUT), (RZ, Q3), (RE, Q1), (LATE, 1), (RE, Q2), (RE, Q3), (LATE, 2),),
}


def mega(comm, *refs):
    refs = list(refs)

    def take(n):
        out = refs[:n]
        del refs[:n]
        return out

    lens, tok_in, cot_in, vis = take(4)
    if comm:
        wq_in, wo_in, w1_in, w2_in = take(4)
        vec_in = take(8)
    else:
        g_in, vpg_in = take(2)
    bo_out, ig_out = take(2)
    if comm:
        gq_out, go_out, g1_out, g2_out, vg_out, vl_out = take(6)
    else:
        dg_out, vg_out, vl_out = take(3)
    G = dict(zip(NAMES, take(8)))
    TK, CT, H1T, H2T, DYT, HB, O = take(7)
    QS = take(4)
    YA, DH, H, DA, BIAS, LSE, VG, VL, VPG, lsem = take(10)
    if comm:
        Z = dict(zip(NAMES[:5], take(5)))
        SB = sibling_rooms(take(2))
        DB, XB, YB = (rooms(take(3)) for _ in range(3))
        ZB, VB, VR, UB, UR, ssem, rsem = take(7)

    grads_of = {"q0": (DA, 0), "q3": (DA, 384), "q1": (G["f0"], 0), "q2": (G["f0"], 768)}

    tok_copy = pltpu.make_async_copy(tok_in, H.at[:, pl.ds(0, D)], lsem.at[0])
    cot_copy = pltpu.make_async_copy(cot_in, DA.at[:, pl.ds(0, D)], lsem.at[1])
    bo_copy = pltpu.make_async_copy(HB, bo_out, lsem.at[0])
    ig_copy = pltpu.make_async_copy(YA, ig_out, lsem.at[1])
    tok_copy.start()
    cot_copy.start()

    if comm:
        c, m, core, others, zs = places()
        cs, cx, cy, cd = (others[r] for r in (1, 2, 4, 6))
        links = Links(ssem, rsem)
        to_s, to_x, to_y, to_d, to_z = (cs, m), (cx, m), (cy, m), (cd, m), [(c, z) for z in zs]
        partners = [(others[r], m) for r in range(1, 8)] + to_z
        barrier = pltpu.get_barrier_semaphore()
        for p in partners:
            pl.semaphore_signal(barrier, inc=1, device_id=p, device_id_type=MESH)

        def mine():
            return rows_of(c)

        def part(n, block, half=None):
            return lambda: G[n].at[rows_of(block) if half is None else half_rows_of(block, half)]

        def both(key, ref, device):
            links.add(key, ref, ref, device)

        def z_seg(n, s):
            if n[0] != "f":
                return lambda: Z[n].at[m]
            return lambda: G[n].at[mine(), lanes_at(s * 1024 + m * 256, 256)]

        z_keys, n_keys, far = {}, {}, {}
        for n in NAMES:
            z_keys[n] = [("z", n, s, d) for s in range(SEGS[n]) for d in range(3)]
            for _, _, s, d in z_keys[n]:
                both(("z", n, s, d), z_seg(n, s), to_z[d])
            both(("x", n), part(n, c), to_x)
            both(("y", n), part(n, c), to_y)
            if n in DIRECT:
                both(("dd", n), part(n, c), to_d)
            else:
                both(("dy", n), part(n, cx, 0), to_y)
                both(("dx", n), part(n, cy, 1), to_x)
            for i, block in enumerate((c, cx, cy, cd)):
                both((f"s{i}", n), part(n, block), to_s)
            far[n] = [("dd", n)] if n in DIRECT else [("dy", n), ("dx", n)]
            n_keys[n] = [(k, n) for k in ("x", "y", "s0", "s1", "s2", "s3")] + far[n]
        for d in range(3):
            both(("v", d), lambda: VPG.at[m], to_z[d])

        def gz(n):
            links.start(*z_keys[n])

        def gm(n):
            links.got(*z_keys[n])
            if n[0] == "q":
                w = ZW[n]
                for t in range(3):
                    G[n][mine(), t * w : (t + 1) * w] = sum(Z[n][z] for z in range(4) if HELD[int(n[1])][z] == t)
            elif n == "o":
                for h in range(2):
                    b, lo, hi = 384 * h, Z[n][2 * h], Z[n][2 * h + 1]
                    G[n][mine(), b : b + 128] = lo[:, 0:128]
                    G[n][mine(), b + 128 : b + 256] = lo[:, 128:256] + hi[:, 0:128]
                    G[n][mine(), b + 256 : b + 384] = hi[:, 128:256]
            if n in DIRECT:
                links.start(*far[n])
            links.start(("x", n), ("y", n), ("s0", n))

        def gdx(n):
            links.got(("x", n))
            if n not in DIRECT:
                links.start(("dy", n))
            links.start(("s1", n))

        def gdy(n):
            links.got(("y", n))
            if n not in DIRECT:
                links.start(("dx", n))
            links.start(("s2", n))

        def gs(n):
            links.got(*far[n])
            links.start(("s3", n))

        def gf(n):
            links.got(*[(f"s{i}", n) for i in range(4)])

        def gone(n):
            links.sent(*z_keys[n], *n_keys[n])

        back = {n: (ref, 0) for n, ref in G.items()}
        back.update(grads_of)

        def z_starts(n, z):
            if n == "o":
                return [128 * (z + lax.div(z, 2))]
            if n[0] == "q":
                return [ZW[n] * by_device(z, [t or 0 for t in HELD[int(n[1])]])]
            return [256 * z, 1024 + 256 * z]

        def mem(n, block, half=None):
            rows = lambda: rows_of(block) if half is None else half_rows_of(block, half)
            return lambda: back[n][0].at[rows(), pl.ds(back[n][1], WIDTH[n])]

        def room(ref, n, half=None):
            if half is None:
                return lambda: ref[n]
            return lambda: ref[n].at[pl.ds(48 * half, 48)]

        def z_from(n, s, d):
            return lambda: back[n][0].at[mine(), lanes_at(back[n][1] + z_starts(n, zs[d])[s], ZW[n])]

        def z_room(n, s, d):
            return lambda: ZB.at[d, :, pl.ds(ZPLACE[n] + ZW[n] * s, ZW[n])]

        r_keys, far_back = {}, {}
        for n in NAMES:
            for i in range(4):
                links.add(("S", n, i), mem(n, 2 * i + 1 - core), lambda n=n, i=i: SB[n].at[pl.ds(96 * i, 96)], to_s)
            if n in DIRECT:
                links.add(("DD", n), mem(n, cd), room(DB, n), to_d)
            else:
                links.add(("DX", n), mem(n, cd, 0), room(DB, n, 0), to_x)
                links.add(("DY", n), mem(n, cd, 1), room(DB, n, 1), to_y)
            far_back[n] = [("DD", n)] if n in DIRECT else [("DX", n), ("DY", n)]
            links.add(("X", n), mem(n, cx), room(XB, n), to_x)
            links.add(("Y", n), mem(n, cy), room(YB, n), to_y)
            r_keys[n] = [("Z", n, s, d) for s in range(SEGS[n]) for d in range(3)]
            for _, _, s, d in r_keys[n]:
                links.add(("Z", n, s, d), z_from(n, s, d), z_room(n, s, d), to_z[d])

        def rS(n):
            links.start(*[("S", n, i) for i in range(4)])

        def rD(n):
            links.got(*[("S", n, i) for i in range(4)])

            def add(block):
                ref = mem(n, block)()
                other = SB[n][rows_of(lax.div(block, 2)), :]
                ref[...] = (ref[...].astype(F32) + other.astype(F32)).astype(BF)

            if n in DIRECT:
                for block in (cx, cy, cd, c):
                    add(block)
                links.start(*far_back[n], ("X", n), ("Y", n))
            else:
                add(cd)
                links.start(*far_back[n])
                for block in (cx, cy, c):
                    add(block)

        def rXa(n):
            links.got(("DX", n))
            t, u = mem(n, cy, 0)(), room(DB, n, 0)()
            t[...] = (t[...].astype(F32) + u[...].astype(F32)).astype(BF)
            links.start(("Y", n))

        def rXb(n):
            links.got(("DY", n))
            t, u = mem(n, cx, 1)(), room(DB, n, 1)()
            t[...] = (t[...].astype(F32) + u[...].astype(F32)).astype(BF)
            links.start(("X", n))

        def rZ(n):
            links.got(("X", n), ("Y", n))
            rooms_in = [XB, YB]
            if n in DIRECT:
                links.got(*far_back[n])
                rooms_in.append(DB)
            t = mem(n, c)()
            t[...] = sum((room(ref, n)()[...].astype(F32) for ref in rooms_in), t[...].astype(F32)).astype(BF)
            links.start(*r_keys[n])

        def rE(n):
            links.got(*r_keys[n])
            k = 128 * FIRST[int(n[1])] if n[0] == "q" else 256 * int(n[1]) if n[0] == "f" else 0
            outs = {"o": [go_out], "q": [gq_out], "f": [g1_out, g2_out]}[n[0]]
            w = ZW[n]
            for s, out in enumerate(outs):
                total = back[n][0][mine(), lanes_at(back[n][1] + z_starts(n, m)[s], w)].astype(F32)
                for d in range(3):
                    total = total + ZB[d, :, ZPLACE[n] + w * s : ZPLACE[n] + w * (s + 1)].astype(F32)
                out[:, k : k + w] = total

        def back_gone(n):
            links.sent(*[("S", n, i) for i in range(4)], *far_back[n], ("X", n), ("Y", n), *r_keys[n])

        v_keys = {}
        for r, (src, buf, rec) in {"e": (VG, VB, VR), "l": (VL, UB, UR)}.items():
            for k in range(1, 8):
                links.add((r, k), lambda src=src: src, lambda rec=rec, k=k: rec.at[k - 1], (others[k], m))
            for d in range(3):
                links.add((r, 8 + d), lambda buf=buf: buf, lambda rec=rec, d=d: rec.at[7 + d], to_z[d])
            v_keys[r] = [[(r, k) for k in range(1, 8)], [(r, 8 + d) for d in range(3)]]

        def rv(r, k):
            src, buf, rec, out = (VG, VB, VR, vg_out) if r == "e" else (VL, UB, UR, vl_out)
            if k > 0:
                links.got(*v_keys[r][k - 1])
            if k == 1:
                buf[...] = sum((rec[i] for i in range(7)), src[...])
            if k < 2:
                links.start(*v_keys[r][k])
            else:
                out[...] = buf[...] + rec[7] + rec[8] + rec[9]

        wq = wq_in[...]
        def shard(g):
            n = f"q{g}"
            off = [
                768 * HELD[g][z] + 128 * FIRST[g] - 576 * z if HELD[g][z] is not None else -4096
                for z in range(4)
            ]
            Z[n][m] = dot(wq, one_hot_cols(576, ZW[n], by_device(m, off))).astype(BF)

        shard(0)
        VPG[m] = pack_vectors([v[...] for v in vec_in])
        pl.semaphore_wait(barrier, len(partners))
        gz("q0")
        links.start(*[("v", d) for d in range(3)])
        for g in (1, 2, 3):
            shard(g)
        Z["o"][m] = dot(wo_in[...], one_hot_cols(192, 256, jnp.where(lax.rem(m, 2) == 0, 0, -64))).astype(BF)
        for j in range(3):
            for s, w in enumerate((w1_in, w2_in)):
                G[f"f{j}"][mine(), lanes_at(s * 1024 + m * 256, 256)] = w[:, j * 256 : (j + 1) * 256]
    else:
        g_copies = [
            pltpu.make_async_copy(g_in.at[:, pl.ds(PLACE[n], WIDTH[n])], G[n], lsem.at[2 + i])
            for i, n in enumerate(NAMES)
        ]
        for k in g_copies:
            k.start()
        VPG[...] = vpg_in[...]

    def serve(*label):
        if not comm:
            return
        table = (gz, gm, gdx, gdy, gs, gf, rS, rD, rXa, rXb, rZ, rE)
        for f, n in SCHEDULE.get(label, ()):
            if f in (EARLY, LATE):
                rv("el"[f - EARLY], n)
            else:
                table[f](NAMES[n])

    def leave(n):
        if comm:
            gone(n)

    def served(count, body, *label):
        hooks = {i: functools.partial(serve, *label, i) for i in range(count) if (*label, i) in SCHEDULE}
        loop(count, body, hooks if comm else None)

    start, ends = longest_start(lens)
    tok_copy.wait()
    cot_copy.wait()
    vis8 = jnp.broadcast_to(vis[...], (8, TOK)).astype(F32).astype(BF)

    def roll_tile(i):
        rows = tile_rows(i, R)
        place = lax.broadcasted_iota(jnp.int32, (R, 1), 0) + i * R + start
        place = jnp.where(place >= TOK, place - TOK, place)
        perm = (lax.broadcasted_iota(jnp.int32, (R, TOK), 1) == place).astype(BF)
        TK[rows, :] = dot(perm, H[:, 0:D]).astype(BF)
        CT[rows, :] = dot(perm, DA[:, 0:D]).astype(BF)
        clip = sum((place >= e).astype(jnp.int32) for e in ends)
        spot = lax.broadcasted_iota(jnp.int32, (R, 1), 0) + lax.rem(i, 2) * R
        key = lax.broadcasted_iota(jnp.int32, (1, HALF), 1)
        far = key + lax.div(i, 2) * HALF + start
        far = jnp.where(far >= TOK, far - TOK, far)
        clip_k = sum((far >= e).astype(jnp.int32) for e in ends)
        whole = lax.broadcasted_iota(jnp.int32, (HALF, TOK), 0) + lax.div(i, 2) * HALF + start
        whole = jnp.where(whole >= TOK, whole - TOK, whole)
        keys = (lax.broadcasted_iota(jnp.int32, (HALF, TOK), 1) == whole).astype(BF)
        seen = dot_nt(vis8, keys)[0:1, :]
        allowed = (clip == clip_k) & ((seen > 0.5) | (key == spot))
        BIAS[lax.div(i, 2), tile_rows(lax.rem(i, 2), R), :] = jnp.where(
            allowed, 0.0, MASKED
        ).astype(BF)

    serve(START)
    serve(PACK)
    served(TOK // R, roll_tile, ROLL)

    if comm:
        links.got(*[("v", d) for d in range(3)])

    def spread(parts):
        return sum(dot(VPG[z][r : r + 1, :], place_of[p]) for z, r, p in parts)

    place_of = [
        (
            (
                lax.broadcasted_iota(jnp.int32, (256, D), 0) + 192 * p
                == lax.broadcasted_iota(jnp.int32, (256, D), 1)
            )
            & (lax.broadcasted_iota(jnp.int32, (256, D), 0) < 192)
        ).astype(BF)
        for p in range(4)
    ]
    each = lambda r: [(z, r, z) for z in range(4)]
    gain1, shift1 = spread(each(0)), spread(each(1))
    bias_q = spread([(0, 2, 0), (0, 3, 1), (1, 2, 2), (1, 3, 3)])
    bias_v = spread([(2, 2, 0), (2, 3, 1), (3, 2, 2), (3, 3, 3)])
    bias_o, gain2, shift2, bias_2 = (spread(each(r)) for r in (4, 5, 6, 7))
    bias_1 = [
        jnp.concatenate([VPG[z][8 + j : 9 + j, :].astype(F32) for z in range(4)], axis=1)
        for j in range(3)
    ]

    serve(VEC)

    def ln1_tile(i):
        rows = tile_rows(i, R)
        xhat, _ = norm_parts(TK[rows, :].astype(F32))
        HB[rows, :] = (xhat * gain1 + shift1).astype(BF)

    served(TOK // R, ln1_tile, LN)
    H1T[...] = HB[...].T
    LSE[...] = jnp.zeros_like(LSE)
    serve(T1)
    VG[...] = jnp.zeros_like(VG)
    VL[...] = jnp.zeros_like(VL)

    def dy_tile(i):
        VG[3:4, 0:D] += jnp.sum(CT[tile_rows(i, R), :].astype(F32), axis=0, keepdims=True)

    loop(TOK // R, dy_tile)
    serve(DY)
    if not comm:
        for k in g_copies:
            k.wait()

    def project(g):
        def tile(i):
            rows = tile_rows(i, 512)
            p = dot(HB[rows, :], G[f"q{g}"][...])
            w = ZW[f"q{g}"]
            cols = slice(128 * FIRST[g], 128 * FIRST[g] + w)
            QS[g][rows, 0:w] = ((p[:, 0:w] + bias_q[:, cols]).astype(BF) * 0.125).astype(BF)
            QS[g][rows, w : 2 * w] = p[:, w : 2 * w].astype(BF)
            QS[g][rows, 2 * w :] = (p[:, 2 * w :] + bias_v[:, cols]).astype(BF)

        loop(TOK // 512, tile)

    lane = lax.broadcasted_iota(jnp.int32, (1, 128), 1)
    sides = [lane < 64, lane >= 64]

    def unit_of(u):
        return lax.div(u, 2), lax.rem(u, 2)

    def two_heads(x):
        return jnp.concatenate([jnp.where(sides[0], x, 0), jnp.where(sides[1], x, 0)], axis=0).astype(BF)

    def twice(x):
        return jnp.concatenate([x, x], axis=0)

    def forward_unit(g):
        def unit(u):
            p, half = unit_of(u)
            rows = tile_rows(half, HALF)
            head = 2 * (FIRST[g] + p)
            k = QS[g][rows, lanes_at(ZW[f"q{g}"] + p * 128, 128)]
            v = QS[g][rows, lanes_at(2 * ZW[f"q{g}"] + p * 128, 128)]
            v1 = jnp.concatenate([v, jnp.ones((HALF, 128), BF)], axis=1)
            for a in range(0, HALF, FORWARD):
                some = pl.ds(pl.multiple_of(half * HALF + a, FORWARD), FORWARD)
                q = QS[g][some, lanes_at(p * 128, 128)]
                s = dot_nt(two_heads(q), k) + twice(BIAS[half, a : a + FORWARD, :].astype(F32))
                top = jnp.max(s, axis=1, keepdims=True)
                out = dot(jnp.exp(s - top).astype(BF), v1)
                even, odd = out[:FORWARD], out[FORWARD:]
                total = jnp.where(sides[0], even[:, 128:], odd[:, 128:])
                O[some, lanes_at((FIRST[g] + p) * 128, 128)] = (
                    jnp.where(sides[0], even[:, :128], odd[:, :128]) / total
                ).astype(BF)
                LSE[some, :] = jnp.where(
                    lane == head,
                    top[:FORWARD] + jnp.log(even[:, 128:]),
                    jnp.where(lane == head + 1, top[FORWARD:] + jnp.log(odd[:, 128:]), LSE[some, :]),
                )

        return unit

    def backward_unit(g):
        def unit(u):
            p, half = unit_of(u)
            rows = tile_rows(half, HALF)
            at_q, at_k, at_v = (lanes_at(b * ZW[f"q{g}"] + p * 128, 128) for b in range(3))
            at_o = lanes_at((FIRST[g] + p) * 128, 128)
            head = 2 * (FIRST[g] + p)
            k, v = QS[g][rows, at_k], QS[g][rows, at_v]
            dk = dv = 0.0
            for a in range(0, HALF, BACKWARD):
                some = pl.ds(pl.multiple_of(half * HALF + a, BACKWARD), BACKWARD)
                q, do = two_heads(QS[g][some, at_q]), two_heads(H[some, at_o])
                both = H[some, at_o].astype(F32) * O[some, at_o].astype(F32)
                pick = lambda which, x: jnp.sum(jnp.where(which, x, 0.0), axis=1, keepdims=True)
                delta = jnp.concatenate([pick(sides[0], both), pick(sides[1], both)], axis=0)
                lse = LSE[some, :]
                lse = jnp.concatenate([pick(lane == head, lse), pick(lane == head + 1, lse)], axis=0)
                s = dot_nt(q, k) + twice(BIAS[half, a : a + BACKWARD, :].astype(F32))
                w = jnp.exp(s - lse)
                ds = (w * (dot_nt(do, v) - delta)).astype(BF)
                w = w.astype(BF)
                dq = dot(ds, k)
                QS[g][some, at_q] = (jnp.where(sides[0], dq[:BACKWARD], dq[BACKWARD:]) * 0.125).astype(BF)
                dk = dk + dot(q.T, ds)
                dv = dv + dot(do.T, w)
            QS[g][rows, at_k] = dk.astype(BF).T
            QS[g][rows, at_v] = dv.astype(BF).T

        return unit

    for g in range(4):
        serve(NEED, Q0 + g)
        project(g)
        serve(PROJECT, g)
        served(2 * PAIRS[g], forward_unit(g), FWD, g)
    serve(NEED, OUT)

    def mixed(rows):
        return TK[rows, :].astype(F32) + dot(O[rows, :], G["o"][...]) + bias_o

    def mix_tile(i):
        rows = tile_rows(i, R)
        x2 = mixed(rows)
        xhat, _ = norm_parts(x2)
        HB[rows, :] = (xhat * gain2 + shift2).astype(BF)

    served(TOK // R, mix_tile, MIX)
    H2T[...] = HB[...].T
    serve(T2)
    DYT[...] = CT[...].T
    serve(T3)

    def feed(j):
        W1 = lambda: G[f"f{j}"][:, 0:1024]
        W2 = lambda: G[f"f{j}"][:, 1024:]
        for rows in (slice(0, 512), slice(512, TOK)):
            act, slope = gelu_parts(dot(HB[rows, :], W1()) + bias_1[j])
            H[rows, :] = act.astype(BF)
            da = (dot(CT[rows, :], W2()) * slope).astype(BF)
            DA[rows, :] = da
            VG[4 + j : 5 + j, :] += jnp.sum(da.astype(F32), axis=0, keepdims=True)
        serve(FEED, j, 0)
        if j == 0:
            YA[...] = dot_nt(H[...], W2())
            DH[...] = dot_nt(DA[...], W1())
        else:
            YA[...] += dot_nt(H[...], W2())
            DH[...] += dot_nt(DA[...], W1())
        serve(FEED, j, 1)

    def feed_grads(j):
        G[f"f{j}"][:, 0:1024] = dot(H2T[...], DA[...]).astype(BF)
        G[f"f{j}"][:, 1024:] = dot(DYT[...], H[...]).astype(BF)

    for j in range(3):
        serve(NEED, F0 + j)
        feed(j)
        leave(f"f{j}")
        feed_grads(j)
        serve(FG, j, 0)
        serve(DONE, F0 + j)

    def end_tile(i):
        rows = tile_rows(i, R)
        x2 = mixed(rows)
        HB[rows, :] = (x2 + YA[rows, :] + bias_2).astype(BF)
        xhat, r = norm_parts(x2)
        dh = DH[rows, :]
        VG[1:2, 0:D] += jnp.sum(dh * xhat, axis=0, keepdims=True)
        VG[2:3, 0:D] += jnp.sum(dh, axis=0, keepdims=True)
        dx2 = CT[rows, :].astype(F32) + norm_back(dh, xhat, r, gain2)
        DH[rows, :] = dx2
        dz = dx2.astype(BF)
        CT[rows, :] = dz
        VG[0:1, 0:D] += jnp.sum(dz.astype(F32), axis=0, keepdims=True)
        H[rows, 0:D] = dot_nt(dz, G["o"][...]).astype(BF)

    served(TOK // R, end_tile, END)
    bo_copy.start()
    if not comm:
        f0_copy = pltpu.make_async_copy(G["f0"], dg_out.at[:, pl.ds(PLACE["f0"], FCW)], lsem.at[2])
        f0_copy.start()
    H2T[...] = O[...].T
    serve(OT)
    leave("o")

    G["o"][...] = dot(H2T[...], CT[...]).astype(BF)
    serve(OG, 0)
    serve(DONE, OUT)
    serve(DONE, END)

    def qkv_grads(g):
        (ref, at), w = grads_of[f"q{g}"], ZW[f"q{g}"]
        ref[0:D, at : at + 3 * w] = dot(H1T[...], QS[g][...]).astype(BF)
        cols = slice(128 * FIRST[g], 128 * FIRST[g] + w)

        def sums(i):
            rows = tile_rows(i, R)
            VL[2:3, cols] += jnp.sum(QS[g][rows, 0:w].astype(F32), axis=0, keepdims=True)
            VL[3:4, cols] += jnp.sum(QS[g][rows, 2 * w :].astype(F32), axis=0, keepdims=True)

        loop(TOK // R, sums)

    for g in range(4):
        served(2 * PAIRS[g], backward_unit(g), BWD, g)
        if g == 1 and comm:
            serve(NEED, RE)
            back_gone("f0")
        if g == 1 and not comm:
            f0_copy.wait()
        qkv_grads(g)
        serve(QG, g)
        serve(DONE, Q0 + g)

    def last_tile(i):
        rows = tile_rows(i, 512)
        dh = sum(dot_nt(QS[g][rows, :], G[f"q{g}"][...]) for g in range(4))
        xhat, r = norm_parts(TK[rows, :].astype(F32))
        VL[0:1, :] += jnp.sum(dh * xhat, axis=0, keepdims=True)
        VL[1:2, :] += jnp.sum(dh, axis=0, keepdims=True)
        YA[rows, :] = DH[rows, :] + norm_back(dh, xhat, r, gain1)

    served(TOK // 512, last_tile, LAST)
    ig_copy.start()
    serve(DONE, LAST)
    serve(NEED, LAST)
    if comm:
        for n in NAMES:
            if n[0] == "q":
                gone(n)
            if n != "f0":
                back_gone(n)
        for r in "el":
            links.sent(*v_keys[r][0], *v_keys[r][1])
        links.sent(*[("v", d) for d in range(3)])
    else:
        vg_out[...] = VG[...]
        vl_out[...] = VL[...]
        last = []
        for i, n in enumerate(NAMES):
            if n == "f0":
                continue
            ref, at = grads_of.get(n, (G[n], 0))
            src = ref.at[pl.ds(0, D), pl.ds(at, WIDTH[n])]
            last.append(pltpu.make_async_copy(src, dg_out.at[:, pl.ds(PLACE[n], WIDTH[n])], lsem.at[2 + i]))
        for k in last:
            k.start()
        for k in last:
            k.wait()
    bo_copy.wait()
    ig_copy.wait()


def run_mega(comm, lens, tok, cot, vis, *rest):
    vm = pl.BlockSpec(memory_space=pltpu.VMEM)
    hbm = pl.BlockSpec(memory_space=pl.ANY)
    smem = pl.BlockSpec(memory_space=pltpu.SMEM)
    S = jax.ShapeDtypeStruct
    V = pltpu.VMEM
    outs = [S((TOK, D), BF), S((TOK, D), F32)]
    out_specs = [hbm, hbm]
    if comm:
        outs += [S((96, D), F32), S((96, 256), F32), S((96, D), F32), S((96, D), F32), S((8, 1024), F32), S((8, D), F32)]
        out_specs += [vm] * 6
    else:
        outs += [S((D, COLS), BF), S((8, 1024), F32), S((8, D), F32)]
        out_specs += [hbm, vm, vm]
    wide, tall, flat = V((TOK, D), BF), V((D, TOK), BF), V((TOK, D), F32)
    scratch = [V((D, WIDTH[n]), BF) for n in NAMES]
    scratch += [wide, wide, tall, tall, tall, wide, wide] + [V((TOK, 384 * n), BF) for n in PAIRS] + [flat, flat]
    scratch += [V((TOK, 1024), BF), V((TOK, 1024), BF), V((2, HALF, HALF), BF), V((TOK, 128), F32)]
    scratch += [V((8, 1024), F32), V((8, D), F32), V((4, 16, 256), BF), pltpu.SemaphoreType.DMA((10,))]
    if comm:
        scratch += [V((4, 96, ZW[n]), BF) for n in NAMES[:5]]
        scratch += [V((384, FCW), BF)] * 2 + [V((96, FCW), BF)] * 9
        scratch += [V((3, 96, ZCOLS), BF), V((8, 1024), F32), V((10, 8, 1024), F32), V((8, D), F32), V((10, 8, D), F32)]
        scratch += [pltpu.SemaphoreType.DMA((224,)), pltpu.SemaphoreType.DMA((224,))]
    return pl.pallas_call(
        functools.partial(mega, comm),
        out_shape=outs,
        in_specs=[smem, hbm, hbm, vm] + ([vm] * 12 if comm else [hbm, vm]),
        out_specs=out_specs,
        scratch_shapes=scratch,
        compiler_params=pltpu.CompilerParams(
            collective_id=0 if comm else None, has_side_effects=comm, vmem_limit_bytes=64 * 2**20
        ),
        cost_estimate=pl.CostEstimate(flops=60 * 10**9, bytes_accessed=20 * 10**6, transcendentals=10**7),
        name="block",
    )(lens, tok, cot, vis, *rest)


def finish(lens, bo_in, ig_in, gq_in, go_in, g1_in, g2_in, vg_in, vl_in, bo, ig, gg1, gs1, gq, gbqv, go, gbo, gg2, gs2, g1, gb1, g2, gb2, twice):
    m = lax.axis_index("mlp")
    start, _ = longest_start(lens)
    first = TOK - start
    low = lax.rem(first, 8)
    window = pl.ds(pl.multiple_of(first - low, 8), TOK + 8)
    for src, dst in ((bo_in, bo), (ig_in, ig)):
        x = src[...].astype(F32)
        twice[0:TOK, :] = x
        twice[TOK : 2 * TOK, :] = x

        def put(k, dst=dst):
            dst[...] = twice[window, :][k : k + TOK].astype(dst.dtype)

        for k in range(8):
            pl.when(low == k)(functools.partial(put, k))

    @pl.when(pl.program_id(0) == 0)
    def _():
        cat = lambda *p: jnp.concatenate(p, axis=1)
        x = gq_in[...]
        p0, p1, p2, p3 = x[:, 0:128], x[:, 128:384], x[:, 384:640], x[:, 640:768]
        gq[...] = by_device(
            m,
            [
                cat(p0, p1, p2[:, 0:192]),
                cat(p2[:, 192:256], p3, p0, p1),
                cat(p2, p3, p0, p1[:, 0:64]),
                cat(p1[:, 64:256], p2, p3),
            ],
        )
        g1[...] = g1_in[...]
        g2[...] = g2_in[...]
        y = go_in[...]
        go[...] = jnp.where(lax.rem(m, 2) == 0, y[:, 0:192], y[:, 64:256])
        v, u = vg_in[...], vl_in[...]
        row = lambda w, r: by_device(m, [w[r : r + 1, 192 * z : 192 * (z + 1)] for z in range(4)])
        for ref, w, r in ((gg1, u, 0), (gs1, u, 1), (gbo, v, 0), (gg2, v, 1), (gs2, v, 2), (gb2, v, 3)):
            ref[...] = row(w, r).reshape(192)
        gbqv[...] = by_device(m, [u[2:3, 0:384], u[2:3, 384:768], u[3:4, 0:384], u[3:4, 384:768]]).reshape(384)
        gb1[...] = cat(
            *[by_device(m, [v[4 + j : 5 + j, 256 * z : 256 * (z + 1)] for z in range(4)]) for j in range(3)]
        ).reshape(768)


def run_finish(lens, bo, ig, gq, go, g1, g2, vg, vl):
    S = jax.ShapeDtypeStruct
    f = lambda *s: S(s, F32)
    outs = [S((TOK, D), BF), f(TOK, D), f(192), f(192), f(96, 576), f(384), f(96, 192), f(192), f(192), f(192), f(96, D), f(768), f(96, D), f(192)]
    tile = pl.BlockSpec((TOK, 384), lambda i: (0, i))
    full = lambda x: pl.BlockSpec(x.shape, lambda i: (0,) * len(x.shape))
    return pl.pallas_call(
        finish,
        grid=(D // 384,),
        out_shape=outs,
        in_specs=[pl.BlockSpec(memory_space=pltpu.SMEM), tile, tile] + [full(x) for x in (gq, go, g1, g2, vg, vl)],
        out_specs=[tile, tile] + [full(x) for x in outs[2:]],
        scratch_shapes=[pltpu.VMEM((2 * TOK + 8, 384), F32)],
        compiler_params=pltpu.CompilerParams(vmem_limit_bytes=60 * 2**20),
        name="finish",
    )(lens, bo, ig, gq, go, g1, g2, vg, vl)


def body_by_collectives(tokens, clip_lengths, vis, vp, w_qkv, w_out, w_fc1, w_fc2, cotangent):
    def whole(x):
        x = lax.all_gather(x, "clips", axis=0, tiled=True)
        return lax.all_gather(x, "mlp", axis=1, tiled=False)

    n, z = w_qkv.shape[0], lax.axis_size("mlp")
    sub = w_fc1.shape[1] // 3
    q = whole(w_qkv).reshape(D, 3, D)
    q = [q[:, :, 128 * a : 128 * (a + b)].reshape(D, -1) for a, b in zip(FIRST, PAIRS)]
    o = whole(w_out).reshape(D, D)
    f = [whole(w).reshape(D, z, 3, sub).transpose(0, 2, 1, 3) for w in (w_fc1, w_fc2.T)]
    g = jnp.concatenate([*q, o, jnp.stack(f, axis=2).reshape(D, 3 * FCW)], axis=1)
    vpg = lax.all_gather(vp, "mlp", axis=0, tiled=False)
    bo, ig, dg, vg, vl = run_mega(False, clip_lengths, tokens, cotangent, vis, g, vpg)
    dg = lax.psum_scatter(dg.astype(F32), "clips", scatter_dimension=0, tiled=True)
    take = lambda n: dg[:, PLACE[n] : PLACE[n] + WIDTH[n]]
    dq = jnp.concatenate([take(f"q{g}").reshape(n, 3, -1) for g in range(4)], axis=2).reshape(n, z, -1)
    do = take("o").reshape(n, z, -1)
    df = dg[:, PLACE["f0"] :].reshape(n, 3, 2, z, sub).transpose(2, 0, 3, 1, 4).reshape(2, n, z, -1)
    cut = lambda x: lax.psum_scatter(x, "mlp", scatter_dimension=1, tiled=False)
    vg, vl = lax.psum((vg, vl), ("clips", "mlp"))
    m = lax.axis_index("mlp")
    part = lambda x: lax.dynamic_slice_in_dim(x, m * (x.shape[0] // z), x.shape[0] // z)
    row = lambda v, r: part(v[r, :D])
    gb1 = part(vg[4:7].reshape(3, z, sub).transpose(1, 0, 2).reshape(-1))
    start, _ = longest_start(clip_lengths)
    return (
        jnp.roll(bo, start, axis=0), jnp.roll(ig, start, axis=0), row(vl, 0), row(vl, 1), cut(dq),
        part(vl[2:4].reshape(-1)), cut(do), row(vg, 0), row(vg, 1), row(vg, 2), cut(df[0]), gb1, cut(df[1]).T, row(vg, 3),
    )


def body(tokens, clip_lengths, visible, ln1_gain, ln1_bias, w_qkv, b_qv, w_out, b_out, ln2_gain, ln2_bias, w_fc1, b_fc1, w_fc2, b_fc2, cotangent):
    vis = visible.reshape(1, TOK)
    vectors = (ln1_gain, ln1_bias, b_qv, b_out, ln2_gain, ln2_bias, b_fc2, b_fc1)
    if (lax.axis_size("clips"), lax.axis_size("mlp")) != (8, 4):
        return body_by_collectives(
            tokens, clip_lengths, vis, pack_vectors(vectors), w_qkv, w_out, w_fc1, w_fc2, cotangent
        )
    bo, ig, gq, go, g1, g2, vg, vl = run_mega(True, clip_lengths, tokens, cotangent, vis, w_qkv, w_out, w_fc1, w_fc2.T, *vectors)
    bo, ig, gg1, gs1, gq, gbqv, go, gbo, gg2, gs2, g1, gb1, g2, gb2 = run_finish(
        clip_lengths, bo, ig, gq, go, g1, g2, vg, vl
    )
    return (bo, ig, gg1, gs1, gq, gbqv, go, gbo, gg2, gs2, g1, gb1, g2.T, gb2)


def solution(mesh):
    in_specs = (
        P(("clips", "mlp"), None), P(("clips", "mlp"), None), P(("clips", "mlp")), P("mlp"), P("mlp"),
        P("clips", "mlp"), P("mlp"), P("clips", "mlp"), P("mlp"), P("mlp"), P("mlp"), P("clips", "mlp"),
        P("mlp"), P("mlp", "clips"), P("mlp"), P(("clips", "mlp"), None),
    )
    out_specs = (
        P(("clips", "mlp"), None), P(("clips", "mlp"), None), P("mlp"), P("mlp"), P("clips", "mlp"), P("mlp"),
        P("clips", "mlp"), P("mlp"), P("mlp"), P("mlp"), P("clips", "mlp"), P("mlp"), P("mlp", "clips"), P("mlp"),
    )
    return jax.shard_map(body, mesh=mesh, in_specs=in_specs, out_specs=out_specs, check_vma=False)
```
